32 devices in a mesh: dp: 8 (over y, x, core), mp: 4 (over z).
Axes of the slice: x: 2, y: 2, z: 4, core: 2. Of those that a mesh axis runs over, the one named last changes fastest.
Arguments:
- image_states: bfloat16 [16, 1024, 1024], P('dp', 'mp'), may hold values from -6 to 6
- text_states: bfloat16 [16, 128, 1024], P('dp'), may hold values from -6 to 6
- text_mask: int32 [16, 128], P('dp'), may hold values from 0 to 1, as said below
- cotangent: bfloat16 [16, 1024, 1024], P('dp', 'mp'), may hold values from -6 to 6
- input_weights: float32 [6, 1024, 1024], P(None, 'dp', 'mp'), may hold values from -0.1875 to 0.1875
- output_weights: float32 [2, 1024, 1024], P(None, 'dp', 'mp'), may hold values from -1 to 1
- hidden_weights: float32 [2, 1024, 4096], P(None, 'dp', 'mp'), may hold values from -0.1875 to 0.1875
- norm_gains: float32 [6, 1024], P(None, ('dp', 'mp')), may hold values from -0.3 to 1.95, as said below
- input_momentum: float32 [6, 1024, 1024], P(None, 'dp', 'mp'), may hold values from -0.0004272461 to 0.0004272461
- output_momentum: float32 [2, 1024, 1024], P(None, 'dp', 'mp'), may hold values from -0.00015258789 to 0.00015258789
- hidden_momentum: float32 [2, 1024, 4096], P(None, 'dp', 'mp'), may hold values from -0.0004272461 to 0.0004272461
- gains_momentum: float32 [6, 1024], P(None, ('dp', 'mp')), may hold values from -0.00030517578 to 0.00030517578
- input_variance: float32 [6, 1024, 1024], P(None, 'dp', 'mp'), may hold values from 1.5258789e-09 to 2.4795533e-08
- output_variance: float32 [2, 1024, 1024], P(None, 'dp', 'mp'), may hold values from 4.768372e-10 to 1.9073487e-09
- hidden_variance: float32 [2, 1024, 4096], P(None, 'dp', 'mp'), may hold values from 1.5258789e-09 to 2.4795533e-08
- gains_variance: float32 [6, 1024], P(None, ('dp', 'mp')), may hold values from 1.9073487e-09 to 1.525879e-08
Outputs:
- layer_out: float32 [16, 1024, 1024], P('dp', 'mp')
- image_gradient: float32 [16, 1024, 1024], P('dp', 'mp')
- text_gradient: float32 [16, 128, 1024], P('dp', 'mp')
- global_norm: float32 [], replicated
- input_updated: float32 [6, 1024, 1024], P(None, 'dp', 'mp')
- output_updated: float32 [2, 1024, 1024], P(None, 'dp', 'mp')
- hidden_updated: float32 [2, 1024, 4096], P(None, 'dp', 'mp')
- gains_updated: float32 [6, 1024], P(None, ('dp', 'mp'))
- input_moment: float32 [6, 1024, 1024], P(None, 'dp', 'mp')
- output_moment: float32 [2, 1024, 1024], P(None, 'dp', 'mp')
- hidden_moment: float32 [2, 1024, 4096], P(None, 'dp', 'mp')
- gains_moment: float32 [6, 1024], P(None, ('dp', 'mp'))
- input_square: float32 [6, 1024, 1024], P(None, 'dp', 'mp')
- output_square: float32 [2, 1024, 1024], P(None, 'dp', 'mp')
- hidden_square: float32 [2, 1024, 4096], P(None, 'dp', 'mp')
- gains_square: float32 [6, 1024], P(None, ('dp', 'mp'))
The draws below stay inside these ranges and needn't reach their ends.
Inputs may be any that keep to these rules, and one draw needn't show every extreme that they name: `text_mask`: each item's row is 1 on its first n positions and 0 after them, with n from 8 to 128; some item has all 128 valid. `norm_gains`: rows 0, 2 and 4 are gains, rows 1, 3 and 5 biases.
All inputs are finite; a program needn't handle non-finite values.
Results may differ from the reference program's by a relative error of at most 0.023.
Values may be sent and summed in bfloat16 or wider, within the bound.
No kernel may reach another device: no remote copies, remote signals or barrier semaphores. Data moves between devices by JAX's collectives and lax.ppermute only.
A program may use at most 192 MiB of HBM per device.

```python
import math
import jax
import jax.numpy as jnp
from jax import lax

D = 1024
HEADS = 16
HEAD_DIM = 64
FF = 4096
SEQ = 1024
TEXT = 128
STEP = 10
ITEMS = 16


def draw_text_mask(key, part):
    lengths = jax.random.randint(jax.random.fold_in(key, 11), (ITEMS,), max(1, TEXT // 16), TEXT + 1)
    chosen = jax.random.randint(jax.random.fold_in(key, 12), (), 0, ITEMS)
    lengths = jnp.where(jnp.arange(ITEMS) == chosen, TEXT, lengths)
    return (jnp.arange(TEXT)[None, :] < lengths[:, None]).astype(jnp.int32)


def draw_norm_gains(key, part):
    spread = jax.random.uniform(jax.random.fold_in(key, 21), (6, D), jnp.float32, -1.0, 1.0)
    place = jnp.arange(D, dtype=jnp.float32)[None, :] / D
    ramp = 0.5 + place
    parity = (jnp.arange(6) % 2)[:, None]
    return jnp.where(parity == 0, ramp * (1.0 + 0.3 * spread), 0.3 * spread)


def levels(key, extent, shards, low, high):
    level = 1.0
    for dim, parts in shards:
        heights = jax.random.uniform(jax.random.fold_in(jax.random.fold_in(key, 6), dim), (parts,), jnp.float32, low / len(shards), high / len(shards))
        level = level * jnp.repeat(jnp.exp(heights), extent[dim] // parts).reshape((-1,) + (1,) * (len(extent) - 1 - dim))
    return level


def centred(own_key, extent, scale, limit, split=(), kind=jnp.bfloat16):
    values = scale * jax.random.normal(own_key, extent, jnp.float32)
    if split:
        values = values * levels(own_key, extent, split, -0.22, 0.18)
    return jnp.clip(values, -limit, limit).astype(kind)


def setup_inputs(seed: int = 0) -> dict:
    key_list = jax.random.split(jax.random.key(seed), 17)
    return {
        "image_states": centred(key_list[0], (ITEMS, SEQ, D), 1.0, 6.0, ((0, 8), (1, 4))),
        "text_states": centred(key_list[1], (ITEMS, TEXT, D), 1.0, 6.0, ((0, 8),)),
        "text_mask": draw_text_mask(jax.random.fold_in(key_list[16], 71), 0),
        "cotangent": centred(key_list[3], (ITEMS, SEQ, D), 1.0, 6.0, ((0, 8), (1, 4))),
        "input_weights": centred(key_list[4], (6, D, D), D ** -0.5, 0.1875, ((1, 8), (2, 4)), jnp.float32),
        "output_weights": centred(key_list[5], (2, D, D), (max(1, 4 * D // TEXT)) ** -0.5, 1.0, ((1, 8), (2, 4)), jnp.float32),
        "hidden_weights": centred(key_list[6], (2, D, FF), D ** -0.5, 0.1875, ((1, 8), (2, 4)), jnp.float32),
        "norm_gains": draw_norm_gains(jax.random.fold_in(key_list[16], 71), 0),
        "input_momentum": centred(key_list[8], (6, D, D), (0.028 / D), 0.0004272461, ((1, 8), (2, 4)), jnp.float32),
        "output_momentum": centred(key_list[9], (2, D, D), (0.011 / D), 0.00015258789, ((1, 8), (2, 4)), jnp.float32),
        "hidden_momentum": centred(key_list[10], (2, D, FF), (0.028 / D), 0.0004272461, ((1, 8), (2, 4)), jnp.float32),
        "gains_momentum": centred(key_list[11], (6, D), (0.022 / D), 0.00030517578, ((1, 32),), jnp.float32),
        "input_variance": jnp.clip(jnp.exp(math.log(2.479553273815327e-08) - 2.78809295 * jax.random.uniform(key_list[12], (6, D, D), jnp.float32) ** levels(key_list[12], (6, D, D), ((1, 8), (2, 4)), -0.2, 0.2)), 1.5258788677030566e-09, 2.479553273815327e-08),
        "output_variance": jnp.clip(jnp.exp(math.log(1.907348723406699e-09) - 1.3862944 * jax.random.uniform(key_list[13], (2, D, D), jnp.float32) ** levels(key_list[13], (2, D, D), ((1, 8), (2, 4)), -0.2, 0.2)), 4.768371808516747e-10, 1.907348723406699e-09),
        "hidden_variance": jnp.clip(jnp.exp(math.log(2.479553273815327e-08) - 2.78809295 * jax.random.uniform(key_list[14], (2, D, FF), jnp.float32) ** levels(key_list[14], (2, D, FF), ((1, 8), (2, 4)), -0.2, 0.2)), 1.5258788677030566e-09, 2.479553273815327e-08),
        "gains_variance": jnp.clip(jnp.exp(math.log(1.525878978725359e-08) - 2.0794415 * jax.random.uniform(key_list[15], (6, D), jnp.float32) ** levels(key_list[15], (6, D), ((1, 32),), -0.2, 0.2)), 1.907348723406699e-09, 1.525878978725359e-08),
    }


@jax.custom_vjp
def low(v):
    return lax.optimization_barrier(v.astype(jnp.bfloat16)).astype(jnp.float32)

@jax.custom_vjp
def low_back(v):
    return v

def low_keep(v):
    return (low(v), None)

def low_pass(kept, grad):
    return (grad,)

def back_keep(v):
    return (v, None)

def back_low(kept, grad):
    return (low(grad),)
low.defvjp(low_keep, low_pass)
low_back.defvjp(back_keep, back_low)
NORM_EPSILON = 1e-05
MASKED_SCORE = -1e+30
BETA_FIRST = 0.9
BETA_SECOND = 0.95
LEARN_RATE = 0.1
GAIN_RATE = 0.5
WEIGHT_DECAY = 0.1
ADAM_EPSILON = 1e-08
CLIP_LIMIT = 1.0
GELU_SCALE = 0.7978845608028654
GELU_CUBIC = 0.044715

def normalize(values, gain_row, shift_row):
    center = values - lax.optimization_barrier(jnp.mean(values, axis=-1, keepdims=True))
    spread = lax.optimization_barrier(jnp.mean(center * center, axis=-1, keepdims=True))
    return center * lax.rsqrt(spread + NORM_EPSILON) * gain_row + shift_row

def gelu_tanh(values):
    return 0.5 * values * (1.0 + jnp.tanh(GELU_SCALE * (values + GELU_CUBIC * values * values * values)))

def matmul(left_side, right_side):
    return jnp.dot(left_side, right_side, precision=lax.Precision.HIGHEST)

def project(row_values, weight):
    return low_back(low(matmul(row_values, weight)))

def attend(queries, key_rows, value_rows, allowed):
    length = queries.shape[0]
    key_count = key_rows.shape[0]
    queries = queries.reshape(length, HEADS, HEAD_DIM)
    key_rows = key_rows.reshape(key_count, HEADS, HEAD_DIM)
    value_rows = value_rows.reshape(key_count, HEADS, HEAD_DIM)
    scores = jnp.einsum('qhe,khe->hqk', queries, key_rows, precision=lax.Precision.HIGHEST)
    scores = low_back(scores * (1.0 / math.sqrt(HEAD_DIM)))
    scores = jnp.where(allowed[None], scores, MASKED_SCORE)
    maximum = lax.optimization_barrier(jnp.max(scores, axis=-1, keepdims=True))
    raised = jnp.exp(scores - maximum)
    weights = low(raised / lax.optimization_barrier(jnp.sum(raised, axis=-1, keepdims=True)))
    mixed_rows = jnp.einsum('hqk,khe->qhe', weights, value_rows, precision=lax.Precision.HIGHEST)
    return low_back(low(mixed_rows.reshape(length, HEADS * HEAD_DIM)))

def item_forward(image_rows, text_rows, text_valid, input_low, output_low, hidden_low, gain_rows):
    length = image_rows.shape[0]
    normed = low(normalize(image_rows, gain_rows[0], gain_rows[1]))
    causal = jnp.arange(length)[:, None] >= jnp.arange(length)[None, :]
    attended = attend(project(normed, input_low[0]), project(normed, input_low[1]), project(normed, input_low[2]), causal)
    first_sum = image_rows + low_back(matmul(attended, output_low[0].T))
    normed = low(normalize(first_sum, gain_rows[2], gain_rows[3]))
    text_allowed = jnp.broadcast_to(text_valid[None, :], (length, text_rows.shape[0]))
    attended = attend(project(normed, input_low[3]), project(text_rows, input_low[4]), project(text_rows, input_low[5]), text_allowed)
    second_sum = first_sum + low_back(matmul(attended, output_low[1].T))
    normed = low(normalize(second_sum, gain_rows[4], gain_rows[5]))
    hidden = low(gelu_tanh(low_back(matmul(normed, hidden_low[0]))))
    return second_sum + low_back(matmul(hidden, hidden_low[1].T))

def adam_update(master, gradient, momentum, variance, factor, rate, decay_rate):
    clipped = gradient * factor
    moment = BETA_FIRST * momentum + (1.0 - BETA_FIRST) * clipped
    square = BETA_SECOND * variance + (1.0 - BETA_SECOND) * clipped * clipped
    step_ratio = moment / (1.0 - BETA_FIRST ** STEP) / (jnp.sqrt(square / (1.0 - BETA_SECOND ** STEP)) + ADAM_EPSILON)
    return (master - rate * (step_ratio + decay_rate * master), moment, square)

def reference(image_states, text_states, text_mask, cotangent, input_weights, output_weights, hidden_weights, norm_gains, input_momentum, output_momentum, hidden_momentum, gains_momentum, input_variance, output_variance, hidden_variance, gains_variance):
    image_float = image_states.astype(jnp.float32)
    text_float = text_states.astype(jnp.float32)
    text_valid = text_mask > 0

    def forward(image_rows, text_rows, input_master, output_master, hidden_master, gain_rows):
        input_low = low(input_master)
        output_low = low(output_master)
        hidden_low = low(hidden_master)

        def one_item(packed):
            return item_forward(packed[0], packed[1], packed[2], input_low, output_low, hidden_low, gain_rows)
        return lax.map(jax.checkpoint(one_item), (image_rows, text_rows, text_valid))
    layer_float, pull_back = jax.vjp(forward, image_float, text_float, input_weights, output_weights, hidden_weights, norm_gains)
    image_gradient, text_gradient, input_gradient, output_gradient, hidden_gradient, gains_gradient = pull_back(cotangent.astype(jnp.float32))
    square_total = jnp.sum(input_gradient * input_gradient) + jnp.sum(output_gradient * output_gradient)
    square_total = square_total + jnp.sum(hidden_gradient * hidden_gradient) + jnp.sum(gains_gradient * gains_gradient)
    global_norm = jnp.sqrt(square_total)
    factor = jnp.minimum(1.0, CLIP_LIMIT / (global_norm + 1e-06))
    input_updated, input_moment, input_square = adam_update(input_weights, input_gradient, input_momentum, input_variance, factor, LEARN_RATE, WEIGHT_DECAY)
    output_updated, output_moment, output_square = adam_update(output_weights, output_gradient, output_momentum, output_variance, factor, LEARN_RATE, WEIGHT_DECAY)
    hidden_updated, hidden_moment, hidden_square = adam_update(hidden_weights, hidden_gradient, hidden_momentum, hidden_variance, factor, LEARN_RATE, WEIGHT_DECAY)
    gains_updated, gains_moment, gains_square = adam_update(norm_gains, gains_gradient, gains_momentum, gains_variance, factor, GAIN_RATE, 0.0)
    return (layer_float, image_gradient, text_gradient, global_norm, input_updated, output_updated, hidden_updated, gains_updated, input_moment, output_moment, hidden_moment, gains_moment, input_square, output_square, hidden_square, gains_square)
```

```python
import math
import jax, jax.numpy as jnp
from jax import lax
from jax.experimental import pallas as pl
from jax.experimental.pallas import tpu as pltpu
BF=jnp.bfloat16; F32=jnp.float32
HEAD_DIM=64; MASKED=-1e30; BQ=256
NT=(((1,),(1,)),((),())); NN=(((1,),(0,)),((),())); TN=(((0,),(0,)),((),()))
def dot(a,b,dims): return lax.dot_general(a,b,dims,preferred_element_type=F32)

def place_of(block, core, half):
    return pl.multiple_of(((block % 2) ^ core) * half + (block // 2) * 128, 128)

def self_fwd_kernel(core_ref, q_ref, k_ref, v_ref, o_ref, l_ref, qs, ks, vs, *, seq):
    core=core_ref[0]; half=seq//2
    for b in range(seq//128):
        at=pl.ds(place_of(b,core,half),128); to=slice(b*128,b*128+128)
        qs[to,:]=(q_ref[at,:].astype(F32)*0.125).astype(BF)
        ks[to,:]=k_ref[at,:]
        vs[to,:]=v_ref[at,:]
    low=lax.broadcasted_iota(jnp.int32,(1,128),1)<HEAD_DIM
    for i in range(seq//BQ):
        n=(i+1)*BQ
        q=qs[i*BQ:n,:]
        outs=[]
        for h in range(2):
            keep=low if h==0 else ~low
            kh=jnp.where(keep,ks[0:n,:],jnp.zeros((),BF))
            s=dot(kh,q,NT)
            tri=lax.broadcasted_iota(jnp.int32,(BQ,BQ),0)<=lax.broadcasted_iota(jnp.int32,(BQ,BQ),1)
            diag=jnp.where(tri,s[n-BQ:,:],MASKED)
            s=diag if n==BQ else jnp.concatenate([s[:n-BQ],diag],0)
            m=jnp.max(s,axis=0,keepdims=True)
            e=jnp.exp(s-m)
            t=jnp.sum(e,axis=0,keepdims=True)
            l_ref[0,h:h+1,i*BQ:n]=m+jnp.log(t)
            vh=vs[0:n,h*64:h*64+64]
            o=dot(vh,e.astype(BF),TN)
            outs.append(o*(1.0/t))
        o=jnp.concatenate(outs,0).T.astype(BF)
        for j in range(BQ//128):
            o_ref[pl.ds(place_of(i*(BQ//128)+j,core,half),128),:]=o[j*128:j*128+128]

def self_bwd_kernel(core_ref, q_ref, k_ref, v_ref, g_ref, l_ref, dq_ref, dk_ref, dv_ref, qs, ks, vs, gs, dka, dva, *, seq):
    core=core_ref[0]; half=seq//2
    for b in range(seq//128):
        at=pl.ds(place_of(b,core,half),128); to=slice(b*128,b*128+128)
        qs[to,:]=(q_ref[at,:].astype(F32)*0.125).astype(BF)
        ks[to,:]=k_ref[at,:]
        vs[to,:]=v_ref[at,:]
        gs[to,:]=g_ref[at,:]
    dka[...]=jnp.zeros_like(dka); dva[...]=jnp.zeros_like(dva)
    low=lax.broadcasted_iota(jnp.int32,(1,128),1)<HEAD_DIM
    zero=jnp.zeros((),BF)
    for i in range(seq//BQ):
        n=(i+1)*BQ; rows=slice(i*BQ,n)
        q=qs[rows,:]; g=gs[rows,:]
        ps=[]; dss=[]
        for h in range(2):
            keep=low if h==0 else ~low
            kh=jnp.where(keep,ks[0:n,:],zero)
            vh=jnp.where(keep,vs[0:n,:],zero)
            s=dot(kh,q,NT)
            tri=lax.broadcasted_iota(jnp.int32,(BQ,BQ),0)<=lax.broadcasted_iota(jnp.int32,(BQ,BQ),1)
            diag=jnp.where(tri,s[n-BQ:,:],MASKED)
            s=diag if n==BQ else jnp.concatenate([s[:n-BQ],diag],0)
            p=jnp.exp(s-l_ref[0,h:h+1,rows])
            dp=dot(vh,g,NT)
            delta=jnp.sum(p*dp,axis=0,keepdims=True)
            ds=(p*(dp-delta)).astype(BF)
            ps.append(p.astype(BF)); dss.append(ds)
        qa=jnp.concatenate([jnp.where(low,q,zero),jnp.where(low,zero,q)],0)
        ga=jnp.concatenate([jnp.where(low,g,zero),jnp.where(low,zero,g)],0)
        dva[0:n,:]+=dot(jnp.concatenate(ps,1),ga,NN)
        dka[0:n,:]+=dot(jnp.concatenate(dss,1),qa,NN)
        k=ks[0:n,:]
        dqt=jnp.concatenate([dot(ks[0:n,0:64],dss[0],TN),dot(ks[0:n,64:128],dss[1],TN)],0)
        dq=(dqt.T*0.125).astype(BF)
        for j in range(BQ//128):
            dq_ref[pl.ds(place_of(i*(BQ//128)+j,core,half),128),:]=dq[j*128:j*128+128]
    for b in range(seq//128):
        at=pl.ds(place_of(b,core,half),128)
        dk_ref[at,:]=dka[b*128:b*128+128,:].astype(BF)
        dv_ref[at,:]=dva[b*128:b*128+128,:].astype(BF)

def cross_fwd_kernel(mask_ref, q_ref, k_ref, v_ref, o_ref, l_ref, *, seq):
    low=lax.broadcasted_iota(jnp.int32,(1,128),1)<HEAD_DIM
    zero=jnp.zeros((),BF)
    valid=mask_ref[:,0:1]>0
    k=k_ref[...]; v=v_ref[...]
    for i in range(seq//BQ):
        rows=slice(i*BQ,(i+1)*BQ)
        q=(q_ref[rows,:].astype(F32)*0.125).astype(BF)
        outs=[]
        for h in range(2):
            kh=jnp.where(low if h==0 else ~low,k,zero)
            s=jnp.where(valid,dot(kh,q,NT),MASKED)
            m=jnp.max(s,axis=0,keepdims=True)
            e=jnp.exp(s-m)
            t=jnp.sum(e,axis=0,keepdims=True)
            l_ref[0,h:h+1,rows]=m+jnp.log(t)
            outs.append(dot(v[:,h*64:h*64+64],e.astype(BF),TN)*(1.0/t))
        o_ref[rows,:]=jnp.concatenate(outs,0).T.astype(BF)

def cross_bwd_kernel(mask_ref, q_ref, k_ref, v_ref, g_ref, l_ref, dq_ref, dk_ref, dv_ref, *, seq):
    low=lax.broadcasted_iota(jnp.int32,(1,128),1)<HEAD_DIM
    zero=jnp.zeros((),BF)
    valid=mask_ref[:,0:1]>0
    k=k_ref[...]; v=v_ref[...]
    dk=jnp.zeros(k.shape,F32); dv=jnp.zeros(k.shape,F32)
    for i in range(seq//BQ):
        rows=slice(i*BQ,(i+1)*BQ)
        q=(q_ref[rows,:].astype(F32)*0.125).astype(BF); g=g_ref[rows,:]
        ps=[]; dss=[]; dqs=[]
        for h in range(2):
            keep=low if h==0 else ~low
            kh=jnp.where(keep,k,zero); vh=jnp.where(keep,v,zero)
            s=jnp.where(valid,dot(kh,q,NT),MASKED)
            p=jnp.exp(s-l_ref[0,h:h+1,rows])
            dp=dot(vh,g,NT)
            delta=jnp.sum(p*dp,axis=0,keepdims=True)
            ds=(p*(dp-delta)).astype(BF)
            ps.append(p.astype(BF)); dss.append(ds)
            dqs.append(dot(k[:,h*64:h*64+64],ds,TN))
        qa=jnp.concatenate([jnp.where(low,q,zero),jnp.where(low,zero,q)],0)
        ga=jnp.concatenate([jnp.where(low,g,zero),jnp.where(low,zero,g)],0)
        dv=dv+dot(jnp.concatenate(ps,1),ga,NN)
        dk=dk+dot(jnp.concatenate(dss,1),qa,NN)
        dq_ref[rows,:]=(jnp.concatenate(dqs,0).T*0.125).astype(BF)
    dk_ref[...]=dk.astype(BF); dv_ref[...]=dv.astype(BF)

def col(rows): return pl.BlockSpec((rows,128),lambda p,*_:(0,p))
LSPEC=pl.BlockSpec((1,2,None),lambda p,*_:(p,0,0))
def params(): return pltpu.CompilerParams(vmem_limit_bytes=40*1024*1024)
def self_fwd(core,q,k,v):
    seq,cols=q.shape; pairs=cols//128
    return pl.pallas_call(lambda *r: self_fwd_kernel(*r,seq=seq),
        grid_spec=pltpu.PrefetchScalarGridSpec(num_scalar_prefetch=1,grid=(pairs,),in_specs=[col(seq)]*3,
            out_specs=[col(seq),pl.BlockSpec((1,2,seq),lambda p,*_:(p,0,0))],scratch_shapes=[pltpu.VMEM((seq,128),BF)]*3),
        out_shape=[jax.ShapeDtypeStruct((seq,cols),BF),jax.ShapeDtypeStruct((pairs,2,seq),F32)],
        compiler_params=params(),
        cost_estimate=pl.CostEstimate(flops=8*seq*seq*cols*2,bytes_accessed=4*seq*cols*2,transcendentals=seq*seq*pairs),name="self_forward")(core,q,k,v)
def self_bwd(core,q,k,v,g,l):
    seq,cols=q.shape; pairs=cols//128
    return pl.pallas_call(lambda *r: self_bwd_kernel(*r,seq=seq),
        grid_spec=pltpu.PrefetchScalarGridSpec(num_scalar_prefetch=1,grid=(pairs,),in_specs=[col(seq)]*4+[pl.BlockSpec((1,2,seq),lambda p,*_:(p,0,0))],
            out_specs=[col(seq)]*3,scratch_shapes=[pltpu.VMEM((seq,128),BF)]*4+[pltpu.VMEM((seq,128),F32)]*2),
        out_shape=[jax.ShapeDtypeStruct((seq,cols),BF)]*3,
        compiler_params=params(),
        cost_estimate=pl.CostEstimate(flops=20*seq*seq*cols*2,bytes_accessed=8*seq*cols*2,transcendentals=seq*seq*pairs),name="self_backward")(core,q,k,v,g,l)
def cross_fwd(mask,q,k,v):
    seq,cols=q.shape; text=k.shape[0]; pairs=cols//128
    return pl.pallas_call(lambda *r: cross_fwd_kernel(*r,seq=seq),grid=(pairs,),
        in_specs=[pl.BlockSpec((text,128),lambda p:(0,0)),col(seq),col(text),col(text)],
        out_specs=[col(seq),pl.BlockSpec((1,2,seq),lambda p:(p,0,0))],
        out_shape=[jax.ShapeDtypeStruct((seq,cols),BF),jax.ShapeDtypeStruct((pairs,2,seq),F32)],
        compiler_params=params(),
        cost_estimate=pl.CostEstimate(flops=8*seq*text*cols*2,bytes_accessed=3*seq*cols*2,transcendentals=seq*text*pairs*2),name="cross_forward")(mask,q,k,v)
def cross_bwd(mask,q,k,v,g,l):
    seq,cols=q.shape; text=k.shape[0]; pairs=cols//128
    return pl.pallas_call(lambda *r: cross_bwd_kernel(*r,seq=seq),grid=(pairs,),
        in_specs=[pl.BlockSpec((text,128),lambda p:(0,0)),col(seq),col(text),col(text),col(seq),pl.BlockSpec((1,2,seq),lambda p:(p,0,0))],
        out_specs=[col(seq),col(text),col(text)],
        out_shape=[jax.ShapeDtypeStruct((seq,cols),BF),jax.ShapeDtypeStruct((text,cols),BF),jax.ShapeDtypeStruct((text,cols),BF)],
        compiler_params=params(),
        cost_estimate=pl.CostEstimate(flops=20*seq*text*cols*2,bytes_accessed=5*seq*cols*2,transcendentals=seq*text*pairs*2),name="cross_backward")(mask,q,k,v,g,l)


from jax.sharding import PartitionSpec as P

STEP=10
NORM_EPSILON = 1e-05
BETA_FIRST = 0.9
BETA_SECOND = 0.95
LEARN_RATE = 0.1
GAIN_RATE = 0.5
WEIGHT_DECAY = 0.1
ADAM_EPSILON = 1e-08
CLIP_LIMIT = 1.0
GELU_SCALE = 0.7978845608028654
GELU_CUBIC = 0.044715

PAIR = [(0, 1), (1, 0), (2, 3), (3, 2)]
MIDDLE = [(1, 2), (2, 1)]
OUTWARD = [(1, 0), (2, 3)]
INWARD = [(0, 1), (3, 2)]
ACROSS = [(0, 2), (1, 3), (2, 0), (3, 1)]


def swap_dp(value, size, bit):
    return lax.ppermute(value, "dp", [(i, i ^ bit) for i in range(size)])


def move_mp(value, pairs):
    return lax.ppermute(value, "mp", pairs)


def adam_update(master, gradient, momentum, variance, factor, rate, decay_rate):
    clipped = gradient * factor
    moment = BETA_FIRST * momentum + (1.0 - BETA_FIRST) * clipped
    square = BETA_SECOND * variance + (1.0 - BETA_SECOND) * clipped * clipped
    step_ratio = (
        moment
        / (1.0 - BETA_FIRST**STEP)
        / (jnp.sqrt(square / (1.0 - BETA_SECOND**STEP)) + ADAM_EPSILON)
    )
    return (master - rate * (step_ratio + decay_rate * master), moment, square)


def norm_parts(values):
    center = values - jnp.mean(values, axis=-1, keepdims=True)
    spread = jnp.mean(center * center, axis=-1, keepdims=True)
    scale = lax.rsqrt(spread + NORM_EPSILON)
    return center * scale, scale


def norm_back(values, grad, gain_row):
    unit, scale = norm_parts(values)
    scaled = grad * gain_row
    back = scale * (
        scaled
        - jnp.mean(scaled, axis=-1, keepdims=True)
        - unit * jnp.mean(scaled * unit, axis=-1, keepdims=True)
    )
    return back, jnp.sum(grad * unit, axis=0), jnp.sum(grad, axis=0)


def per_device(
    image_states, text_states, text_mask, cotangent,
    input_weights, output_weights, hidden_weights, norm_gains,
    input_momentum, output_momentum, hidden_momentum, gains_momentum,
    input_variance, output_variance, hidden_variance, gains_variance,
):
    size = lax.axis_size("dp")
    lines = lax.axis_size("mp")
    dp = lax.axis_index("dp")
    mp = lax.axis_index("mp")
    core = dp % 2
    chip = dp // 2
    chips = size // 2
    middle = (mp == 1) | (mp == 2)
    bits = []
    bit = 2
    while bit < size:
        bits.append(bit)
        bit *= 2
    width = image_states.shape[-1]
    block = width // chips
    part = width // size

    def pick(first, second):
        return jnp.where(core == 0, first, second)

    def swap_core(value):
        return swap_dp(value, size, 1)

    def reorder(value):
        return jnp.concatenate(
            [lax.dynamic_slice_in_dim(value, (chip ^ p) * block, block, value.ndim - 1) for p in range(chips)], -1
        )

    def own_half(stack):
        half = stack.shape[-1] // 2
        keep = lax.dynamic_slice_in_dim(stack, core * half, half, 2)
        send = lax.dynamic_slice_in_dim(stack, (1 - core) * half, half, 2)
        recv = swap_core(send)
        return jnp.stack([pick(keep, recv), pick(recv, keep)], 1)

    def gather_line(own):
        beside = move_mp(own, PAIR)
        near = jnp.concatenate([own, beside], -1)
        far = move_mp(near, MIDDLE)
        outer = move_mp(far, OUTWARD)
        return jnp.concatenate([near, jnp.where(middle, far, outer)], -1)

    def gather_chips(own, order):
        found = {0: own}
        for b in order:
            codes = sorted(found)
            sent = found[codes[0]] if len(codes) == 1 else jnp.concatenate([found[c] for c in codes], 1)
            got = swap_dp(sent, size, b)
            rows = own.shape[1]
            for i, c in enumerate(codes):
                found[c ^ b] = lax.slice_in_dim(got, i * rows, (i + 1) * rows, axis=1)
        return found

    def gather_group(own):
        line = gather_line(own)
        first = gather_chips(line[:, 0], bits[::-1])
        second = gather_chips(line[:, 1], bits)
        pieces = []
        for p in range(chips):
            pieces += [first[2 * p], second[2 * p]]
        return jnp.concatenate(pieces, 1)

    def scatter_chips(found, order):
        for b in reversed(order):
            codes = sorted(c for c in found if not c & b)
            sent = jnp.concatenate([found[c ^ b] for c in codes], 1)
            got = swap_dp(sent, size, b)
            found = {
                c: found[c] + lax.slice_in_dim(got, i * part, (i + 1) * part, axis=1) for i, c in enumerate(codes)
            }
        return found[0]

    def scatter_line(total):
        half = total.shape[-1] // 2
        near, away = total[..., :half], total[..., half:]
        away = away + move_mp(away, INWARD)
        near = near + move_mp(away, MIDDLE)
        quarter = half // 2
        return near[..., :quarter] + move_mp(near[..., quarter:], PAIR)

    def scatter_group(grad):
        pieces = {}
        for p in range(chips):
            for h in range(2):
                pieces[2 * p, h] = lax.slice_in_dim(grad, (2 * p + h) * part, (2 * p + h + 1) * part, axis=1)
        first = scatter_chips({2 * p: pieces[2 * p, 0] for p in range(chips)}, bits[::-1])
        second = scatter_chips({2 * p: pieces[2 * p, 1] for p in range(chips)}, bits)
        mine = scatter_line(jnp.stack([first, second], 1))
        keep = pick(mine[:, 0], mine[:, 1])
        recv = swap_core(pick(mine[:, 1], mine[:, 0]))
        return jnp.concatenate([pick(keep, recv), pick(recv, keep)], -1).astype(F32)

    items = image_states.shape[0]
    run = image_states.shape[1] // 2

    def bring(value):
        blocks = value.reshape(items, 2, run, width)
        keep = pick(blocks[:, 0], blocks[:, 1])
        recv = swap_core(pick(blocks[:, 1], blocks[:, 0]))
        whole = jnp.concatenate([pick(keep, recv), pick(recv, keep)], 0)
        return reorder(lax.all_to_all(whole, "mp", 0, 0, tiled=True).reshape(lines * run, width))

    def give(value, rows):
        whole = lax.all_to_all(reorder(value).reshape(lines, rows, width), "mp", 0, 0, tiled=True)
        low, high = whole[:items], whole[items:]
        keep = pick(low, high)
        recv = swap_core(pick(high, low))
        return jnp.stack([pick(keep, recv), pick(recv, keep)], 1).reshape(items, 2 * rows, width).astype(F32)

    def both(value):
        return jnp.concatenate([value, swap_core(value)], 0)

    def joined(left, right, dims):
        half = left.shape[0] // 2
        other = dot(left[half:], right, dims).astype(BF)
        return dot(left[:half], right, dims) + swap_core(other).astype(F32)

    low_inout = own_half(jnp.concatenate([input_weights[:3], output_weights[:1], input_weights[3:], output_weights[1:]], 0).astype(BF))
    low_hidden = own_half(hidden_weights.astype(BF))

    gains_all = lax.dynamic_update_slice(
        jnp.zeros((6, width), F32), norm_gains, (0, (dp * lines + mp) * norm_gains.shape[1])
    )

    def sum_all(value):
        bit = 1
        while bit < size:
            value = value + swap_dp(value, size, bit)
            bit *= 2
        value = value + move_mp(value, PAIR)
        return value + move_mp(value, ACROSS)

    gain_rows = reorder(sum_all(gains_all))
    image_own = bring(image_states).astype(F32)

    weights_self = gather_group(low_inout[:4])
    weights_cross = gather_group(low_inout[4:])
    weights_up = gather_group(low_hidden[:1])[0]
    weights_down = gather_group(low_hidden[1:])[0]

    cot_own = bring(cotangent)

    which = mp % items
    mine = lax.dynamic_index_in_dim(text_states, which, 0, keepdims=False)
    mine_mask = lax.dynamic_index_in_dim(text_mask, which, 0, keepdims=False).astype(F32)
    here = (mp // items) == core
    text = reorder(jnp.where(here, mine, swap_core(mine)))
    valid = jnp.where(here, mine_mask, swap_core(mine_mask))
    valid = jnp.broadcast_to(valid[:, None], (valid.shape[0], 128))

    core_index = core.astype(jnp.int32).reshape(1)

    unit, _ = norm_parts(image_own)
    h1 = both((unit * gain_rows[0] + gain_rows[1]).astype(BF))
    q1, k1, v1 = (dot(h1, weights_self[j], NN).astype(BF) for j in range(3))
    o1, l1 = self_fwd(core_index, q1, k1, v1)
    r1 = image_own + joined(o1, weights_self[3], NT)
    unit, _ = norm_parts(r1)
    h2 = both((unit * gain_rows[2] + gain_rows[3]).astype(BF))
    q2 = dot(h2, weights_cross[0], NN).astype(BF)
    k2, v2 = (dot(text, weights_cross[j], NN).astype(BF) for j in (1, 2))
    o2, l2 = cross_fwd(valid, q2, k2, v2)
    r2 = r1 + joined(o2, weights_cross[3], NT)
    unit, _ = norm_parts(r2)
    h3 = both((unit * gain_rows[4] + gain_rows[5]).astype(BF))
    u = dot(h3, weights_up, NN)
    bend = jnp.tanh(GELU_SCALE * (u + GELU_CUBIC * u * u * u))
    e = (0.5 * u * (1.0 + bend)).astype(BF)
    slope = (
        0.5 * (1.0 + bend) + 0.5 * u * (1.0 - bend * bend) * GELU_SCALE * (1.0 + 3.0 * GELU_CUBIC * u * u)
    ).astype(BF)
    layer_own = r2 + joined(e, weights_down, NT)
    layer_out = give(layer_own.astype(BF), run)

    cot = both(cot_own)
    cot_float = cot_own.astype(F32)
    grad_down = dot(cot, e, TN).astype(BF)
    shard_down = scatter_group(grad_down[None])
    du = (dot(cot, weights_down, NN) * slope.astype(F32)).astype(BF)
    grad_up = dot(h3, du, TN).astype(BF)
    shard_up = scatter_group(grad_up[None])
    dh3 = joined(du, weights_up, NT)
    back, gain_five, shift_six = norm_back(r2, dh3, gain_rows[4])
    dr2 = cot_float + back
    z2 = both(dr2.astype(BF))
    do2 = dot(z2, weights_cross[3], NN).astype(BF)
    go1 = dot(z2, o2, TN).astype(BF)
    dq2, dk2, dv2 = cross_bwd(valid, q2, k2, v2, do2, l2)
    dh2 = joined(dq2, weights_cross[0], NT)
    gi3 = dot(h2, dq2, TN).astype(BF)
    gi4 = dot(text, dk2, TN).astype(BF)
    gi5 = dot(text, dv2, TN).astype(BF)
    shard_cross = scatter_group(jnp.stack([gi3, gi4, gi5, go1]))
    text_part = dot(dk2, weights_cross[1], NT) + dot(dv2, weights_cross[2], NT)
    share = text.shape[0] // (2 * lines)
    text_part = text_part.reshape(lines, 2, share, width)
    text_own = pick(text_part[:, 0], text_part[:, 1]) + swap_core(
        pick(text_part[:, 1], text_part[:, 0]).astype(BF)
    ).astype(F32)
    text_gradient = give(text_own.astype(BF).reshape(lines * share, width), share)
    back, gain_three, shift_four = norm_back(r1, dh2, gain_rows[2])
    dr1 = dr2 + back
    z1 = both(dr1.astype(BF))
    do1 = dot(z1, weights_self[3], NN).astype(BF)
    go0 = dot(z1, o1, TN).astype(BF)
    dq1, dk1, dv1 = self_bwd(core_index, q1, k1, v1, do1, l1)
    gi0, gi1, gi2 = (dot(h1, g, TN).astype(BF) for g in (dq1, dk1, dv1))
    shard_self = scatter_group(jnp.stack([gi0, gi1, gi2, go0]))
    half = dq1.shape[0] // 2

    def three(at):
        return (
            dot(dq1[at], weights_self[0], NT) + dot(dk1[at], weights_self[1], NT) + dot(dv1[at], weights_self[2], NT)
        )

    dh1 = three(slice(0, half)) + swap_core(three(slice(half, None)).astype(BF)).astype(F32)
    back, gain_one, shift_two = norm_back(image_own, dh1, gain_rows[0])
    image_gradient = give((dr1 + back).astype(BF), run)

    gains_total = sum_all(reorder(jnp.stack([gain_one, shift_two, gain_three, shift_four, gain_five, shift_six])))
    gains_shard = lax.dynamic_slice_in_dim(
        gains_total, (dp * lines + mp) * norm_gains.shape[1], norm_gains.shape[1], 1
    )

    input_shard = jnp.concatenate([shard_self[:3], shard_cross[:3]], 0)
    output_shard = jnp.concatenate([shard_self[3:], shard_cross[3:]], 0)
    hidden_shard = jnp.concatenate([shard_up, shard_down], 0)
    square_total = jnp.sum(input_shard * input_shard) + jnp.sum(output_shard * output_shard)
    square_total = square_total + jnp.sum(hidden_shard * hidden_shard) + jnp.sum(gains_shard * gains_shard)
    global_norm = jnp.sqrt(sum_all(jnp.full((8, 128), square_total)))[0, 0]
    factor = jnp.minimum(1.0, CLIP_LIMIT / (global_norm + 1e-06))
    input_updated, input_moment, input_square = adam_update(
        input_weights, input_shard, input_momentum, input_variance, factor, LEARN_RATE, WEIGHT_DECAY
    )
    output_updated, output_moment, output_square = adam_update(
        output_weights, output_shard, output_momentum, output_variance, factor, LEARN_RATE, WEIGHT_DECAY
    )
    hidden_updated, hidden_moment, hidden_square = adam_update(
        hidden_weights, hidden_shard, hidden_momentum, hidden_variance, factor, LEARN_RATE, WEIGHT_DECAY
    )
    gains_updated, gains_moment, gains_square = adam_update(
        norm_gains, gains_shard, gains_momentum, gains_variance, factor, GAIN_RATE, 0.0
    )
    return (
        layer_out, image_gradient, text_gradient, global_norm,
        input_updated, output_updated, hidden_updated, gains_updated,
        input_moment, output_moment, hidden_moment, gains_moment,
        input_square, output_square, hidden_square, gains_square,
    )


def solution(mesh):
    rows, weight, gains = P("dp", "mp", None), P(None, "dp", "mp"), P(None, ("dp", "mp"))
    return jax.shard_map(
        per_device,
        mesh=mesh,
        in_specs=(rows, P("dp", None, None), P("dp", None), rows) + (weight, weight, weight, gains) * 3,
        out_specs=(rows, rows, rows, P()) + (weight, weight, weight, gains) * 3,
        check_vma=False,
    )
```

```python
import math
import jax, jax.numpy as jnp
from jax import lax
from jax.experimental import pallas as pl
from jax.experimental.pallas import tpu as pltpu
BF=jnp.bfloat16; F32=jnp.float32
HEAD_DIM=64; MASKED=-1e30; BQ=256
NT=(((1,),(1,)),((),())); NN=(((1,),(0,)),((),())); TN=(((0,),(0,)),((),()))
TINY=pl.CostEstimate(flops=1,bytes_accessed=1,transcendentals=0)
def dot(a,b,dims): return lax.dot_general(a,b,dims,preferred_element_type=F32)

def place_of(block, core, half):
    return pl.multiple_of(((block % 2) ^ core) * half + (block // 2) * 128, 128)

def self_fwd_kernel(core_ref, q_ref, k_ref, v_ref, o_ref, l_ref, qs, ks, vs, *, seq):
    core=core_ref[0]; half=seq//2
    for b in range(seq//128):
        at=pl.ds(place_of(b,core,half),128); to=slice(b*128,b*128+128)
        qs[to,:]=(q_ref[at,:].astype(F32)*0.125).astype(BF)
        ks[to,:]=k_ref[at,:]
        vs[to,:]=v_ref[at,:]
    low=lax.broadcasted_iota(jnp.int32,(1,128),1)<HEAD_DIM
    for i in range(seq//BQ):
        n=(i+1)*BQ
        q=qs[i*BQ:n,:]
        outs=[]
        for h in range(2):
            keep=low if h==0 else ~low
            kh=jnp.where(keep,ks[0:n,:],jnp.zeros((),BF))
            s=dot(kh,q,NT)
            tri=lax.broadcasted_iota(jnp.int32,(BQ,BQ),0)<=lax.broadcasted_iota(jnp.int32,(BQ,BQ),1)
            diag=jnp.where(tri,s[n-BQ:,:],MASKED)
            s=diag if n==BQ else jnp.concatenate([s[:n-BQ],diag],0)
            m=jnp.max(s,axis=0,keepdims=True)
            e=jnp.exp(s-m)
            t=jnp.sum(e,axis=0,keepdims=True)
            l_ref[0,h:h+1,i*BQ:n]=m+jnp.log(t)
            vh=vs[0:n,h*64:h*64+64]
            o=dot(vh,e.astype(BF),TN)
            outs.append(o*(1.0/t))
        o=jnp.concatenate(outs,0).T.astype(BF)
        for j in range(BQ//128):
            o_ref[pl.ds(place_of(i*(BQ//128)+j,core,half),128),:]=o[j*128:j*128+128]

def self_bwd_kernel(core_ref, q_ref, k_ref, v_ref, g_ref, l_ref, dq_ref, dk_ref, dv_ref, qs, ks, vs, gs, dka, dva, *, seq):
    core=core_ref[0]; half=seq//2
    for b in range(seq//128):
        at=pl.ds(place_of(b,core,half),128); to=slice(b*128,b*128+128)
        qs[to,:]=(q_ref[at,:].astype(F32)*0.125).astype(BF)
        ks[to,:]=k_ref[at,:]
        vs[to,:]=v_ref[at,:]
        gs[to,:]=g_ref[at,:]
    dka[...]=jnp.zeros_like(dka); dva[...]=jnp.zeros_like(dva)
    low=lax.broadcasted_iota(jnp.int32,(1,128),1)<HEAD_DIM
    zero=jnp.zeros((),BF)
    for i in range(seq//BQ):
        n=(i+1)*BQ; rows=slice(i*BQ,n)
        q=qs[rows,:]; g=gs[rows,:]
        ps=[]; dss=[]
        for h in range(2):
            keep=low if h==0 else ~low
            kh=jnp.where(keep,ks[0:n,:],zero)
            vh=jnp.where(keep,vs[0:n,:],zero)
            s=dot(kh,q,NT)
            tri=lax.broadcasted_iota(jnp.int32,(BQ,BQ),0)<=lax.broadcasted_iota(jnp.int32,(BQ,BQ),1)
            diag=jnp.where(tri,s[n-BQ:,:],MASKED)
            s=diag if n==BQ else jnp.concatenate([s[:n-BQ],diag],0)
            p=jnp.exp(s-l_ref[0,h:h+1,rows])
            dp=dot(vh,g,NT)
            delta=jnp.sum(p*dp,axis=0,keepdims=True)
            ds=(p*(dp-delta)).astype(BF)
            ps.append(p.astype(BF)); dss.append(ds)
        qa=jnp.concatenate([jnp.where(low,q,zero),jnp.where(low,zero,q)],0)
        ga=jnp.concatenate([jnp.where(low,g,zero),jnp.where(low,zero,g)],0)
        dva[0:n,:]+=dot(jnp.concatenate(ps,1),ga,NN)
        dka[0:n,:]+=dot(jnp.concatenate(dss,1),qa,NN)
        k=ks[0:n,:]
        dqt=jnp.concatenate([dot(ks[0:n,0:64],dss[0],TN),dot(ks[0:n,64:128],dss[1],TN)],0)
        dq=(dqt.T*0.125).astype(BF)
        for j in range(BQ//128):
            dq_ref[pl.ds(place_of(i*(BQ//128)+j,core,half),128),:]=dq[j*128:j*128+128]
    for b in range(seq//128):
        at=pl.ds(place_of(b,core,half),128)
        dk_ref[at,:]=dka[b*128:b*128+128,:].astype(BF)
        dv_ref[at,:]=dva[b*128:b*128+128,:].astype(BF)

def cross_fwd_kernel(mask_ref, q_ref, k_ref, v_ref, o_ref, l_ref, *, seq):
    low=lax.broadcasted_iota(jnp.int32,(1,128),1)<HEAD_DIM
    zero=jnp.zeros((),BF)
    valid=mask_ref[:,0:1]>0
    k=k_ref[...]; v=v_ref[...]
    for i in range(seq//BQ):
        rows=slice(i*BQ,(i+1)*BQ)
        q=(q_ref[rows,:].astype(F32)*0.125).astype(BF)
        outs=[]
        for h in range(2):
            kh=jnp.where(low if h==0 else ~low,k,zero)
            s=jnp.where(valid,dot(kh,q,NT),MASKED)
            m=jnp.max(s,axis=0,keepdims=True)
            e=jnp.exp(s-m)
            t=jnp.sum(e,axis=0,keepdims=True)
            l_ref[0,h:h+1,rows]=m+jnp.log(t)
            outs.append(dot(v[:,h*64:h*64+64],e.astype(BF),TN)*(1.0/t))
        o_ref[rows,:]=jnp.concatenate(outs,0).T.astype(BF)

def cross_bwd_kernel(mask_ref, q_ref, k_ref, v_ref, g_ref, l_ref, dq_ref, dk_ref, dv_ref, *, seq):
    low=lax.broadcasted_iota(jnp.int32,(1,128),1)<HEAD_DIM
    zero=jnp.zeros((),BF)
    valid=mask_ref[:,0:1]>0
    k=k_ref[...]; v=v_ref[...]
    dk=jnp.zeros(k.shape,F32); dv=jnp.zeros(k.shape,F32)
    for i in range(seq//BQ):
        rows=slice(i*BQ,(i+1)*BQ)
        q=(q_ref[rows,:].astype(F32)*0.125).astype(BF); g=g_ref[rows,:]
        ps=[]; dss=[]; dqs=[]
        for h in range(2):
            keep=low if h==0 else ~low
            kh=jnp.where(keep,k,zero); vh=jnp.where(keep,v,zero)
            s=jnp.where(valid,dot(kh,q,NT),MASKED)
            p=jnp.exp(s-l_ref[0,h:h+1,rows])
            dp=dot(vh,g,NT)
            delta=jnp.sum(p*dp,axis=0,keepdims=True)
            ds=(p*(dp-delta)).astype(BF)
            ps.append(p.astype(BF)); dss.append(ds)
            dqs.append(dot(k[:,h*64:h*64+64],ds,TN))
        qa=jnp.concatenate([jnp.where(low,q,zero),jnp.where(low,zero,q)],0)
        ga=jnp.concatenate([jnp.where(low,g,zero),jnp.where(low,zero,g)],0)
        dv=dv+dot(jnp.concatenate(ps,1),ga,NN)
        dk=dk+dot(jnp.concatenate(dss,1),qa,NN)
        dq_ref[rows,:]=(jnp.concatenate(dqs,0).T*0.125).astype(BF)
    dk_ref[...]=dk.astype(BF); dv_ref[...]=dv.astype(BF)

def col(rows): return pl.BlockSpec((rows,128),lambda p,*_:(0,p))
LSPEC=pl.BlockSpec((1,2,None),lambda p,*_:(p,0,0))
def params(): return pltpu.CompilerParams(vmem_limit_bytes=40*1024*1024)
def self_fwd(core,q,k,v):
    seq,cols=q.shape; pairs=cols//128
    return pl.pallas_call(lambda *r: self_fwd_kernel(*r,seq=seq),
        grid_spec=pltpu.PrefetchScalarGridSpec(num_scalar_prefetch=1,grid=(pairs,),in_specs=[col(seq)]*3,
            out_specs=[col(seq),pl.BlockSpec((1,2,seq),lambda p,*_:(p,0,0))],scratch_shapes=[pltpu.VMEM((seq,128),BF)]*3),
        out_shape=[jax.ShapeDtypeStruct((seq,cols),BF),jax.ShapeDtypeStruct((pairs,2,seq),F32)],
        compiler_params=params(),
        cost_estimate=TINY,name="self_forward")(core,q,k,v)
def self_bwd(core,q,k,v,g,l):
    seq,cols=q.shape; pairs=cols//128
    return pl.pallas_call(lambda *r: self_bwd_kernel(*r,seq=seq),
        grid_spec=pltpu.PrefetchScalarGridSpec(num_scalar_prefetch=1,grid=(pairs,),in_specs=[col(seq)]*4+[pl.BlockSpec((1,2,seq),lambda p,*_:(p,0,0))],
            out_specs=[col(seq)]*3,scratch_shapes=[pltpu.VMEM((seq,128),BF)]*4+[pltpu.VMEM((seq,128),F32)]*2),
        out_shape=[jax.ShapeDtypeStruct((seq,cols),BF)]*3,
        compiler_params=params(),
        cost_estimate=TINY,name="self_backward")(core,q,k,v,g,l)
def cross_fwd(mask,q,k,v):
    seq,cols=q.shape; text=k.shape[0]; pairs=cols//128
    return pl.pallas_call(lambda *r: cross_fwd_kernel(*r,seq=seq),grid=(pairs,),
        in_specs=[pl.BlockSpec((text,128),lambda p:(0,0)),col(seq),col(text),col(text)],
        out_specs=[col(seq),pl.BlockSpec((1,2,seq),lambda p:(p,0,0))],
        out_shape=[jax.ShapeDtypeStruct((seq,cols),BF),jax.ShapeDtypeStruct((pairs,2,seq),F32)],
        compiler_params=params(),
        cost_estimate=TINY,name="cross_forward")(mask,q,k,v)
def cross_bwd(mask,q,k,v,g,l):
    seq,cols=q.shape; text=k.shape[0]; pairs=cols//128
    return pl.pallas_call(lambda *r: cross_bwd_kernel(*r,seq=seq),grid=(pairs,),
        in_specs=[pl.BlockSpec((text,128),lambda p:(0,0)),col(seq),col(text),col(text),col(seq),pl.BlockSpec((1,2,seq),lambda p:(p,0,0))],
        out_specs=[col(seq),col(text),col(text)],
        out_shape=[jax.ShapeDtypeStruct((seq,cols),BF),jax.ShapeDtypeStruct((text,cols),BF),jax.ShapeDtypeStruct((text,cols),BF)],
        compiler_params=params(),
        cost_estimate=TINY,name="cross_backward")(mask,q,k,v,g,l)

def split_halves(a,b):
    half,m,rows,cols=a.shape[0]//2,*a.shape[1:]
    def body(a_ref,b_ref,x_ref,y_ref):
        x_ref[...]=a_ref[...]
        y_ref[...]=b_ref[...]
    block=(half,1,rows,cols)
    out=jax.ShapeDtypeStruct((half,m,rows,cols),a.dtype)
    return pl.pallas_call(body,grid=(m,),
        in_specs=[pl.BlockSpec(block,lambda i:(0,i,0,0)),pl.BlockSpec(block,lambda i:(1,i,0,0))],
        out_specs=[pl.BlockSpec(block,lambda i:(0,i,0,0))]*2,out_shape=[out,out],compiler_params=params(),
        cost_estimate=TINY,name="split_halves")(a,b)

def place_pieces(groups,rows):
    first=groups[0][0]
    _,m,_,cols=first.shape
    width=sum(v.shape[0] for v in groups[0])*cols
    flat=[v for g in groups for v in g]
    shapes=[[v.shape[0] for v in g] for g in groups]
    def body(*refs):
        ins,out=refs[:len(flat)],refs[len(flat)]
        at=0
        for p,s in enumerate(shapes):
            def fill(at=at,s=s):
                z=0
                for i,k in enumerate(s):
                    for j in range(k):
                        out[:,:,z*cols:(z+1)*cols]=ins[at+i][j,:,0:rows,:]; z+=1
            pl.when(pl.program_id(0)==p)(fill)
            at+=len(s)
    return pl.pallas_call(body,grid=(len(groups),),
        in_specs=[pl.BlockSpec(v.shape,lambda p:(0,0,0,0),pipeline_mode=pl.Buffered(1)) for v in flat],
        out_specs=pl.BlockSpec((m,rows,width),lambda p:(0,p,0)),
        out_shape=jax.ShapeDtypeStruct((m,rows*len(groups),width),first.dtype),compiler_params=params(),
        cost_estimate=TINY,name="place_pieces")(*flat)

def hidden_up_kernel(h_ref, w_ref, e_ref, s_ref):
    w=w_ref[0]
    for i in range(h_ref.shape[0]//256):
        rows=slice(i*256,(i+1)*256)
        u=dot(h_ref[rows,:],w,NN)
        uu=u*u
        t=jnp.tanh(u*(0.7978845608028654+(0.7978845608028654*0.044715)*uu))
        p=0.5+0.5*t
        e_ref[rows,:]=(u*p).astype(BF)
        s_ref[rows,:]=(p+u*(p*(1.0-t))*(0.7978845608028654+(3.0*0.7978845608028654*0.044715)*uu)).astype(BF)

def hidden_up(h,w):
    rows,depth=h.shape; parts,_,cols=w.shape; blk=256; per=cols//blk
    out=pl.BlockSpec((rows,blk),lambda j:(0,j))
    return pl.pallas_call(hidden_up_kernel,grid=(parts*per,),
        in_specs=[pl.BlockSpec((rows,depth),lambda j:(0,0)),pl.BlockSpec((1,depth,blk),lambda j:(j//per,0,j%per))],
        out_specs=[out,out],out_shape=[jax.ShapeDtypeStruct((rows,parts*cols),BF)]*2,compiler_params=params(),
        cost_estimate=TINY,name="hidden_up")(h,w)

def hidden_slope_kernel(g_ref, w_ref, s_ref, d_ref):
    w=w_ref[0]
    for i in range(g_ref.shape[0]//256):
        rows=slice(i*256,(i+1)*256)
        d_ref[rows,:]=(dot(g_ref[rows,:],w,NN)*s_ref[rows,:].astype(F32)).astype(BF)

def hidden_slope(g,w,s):
    rows,depth=g.shape; parts,_,cols=w.shape; blk=256; per=cols//blk
    out=pl.BlockSpec((rows,blk),lambda j:(0,j))
    return pl.pallas_call(hidden_slope_kernel,grid=(parts*per,),
        in_specs=[pl.BlockSpec((rows,depth),lambda j:(0,0)),pl.BlockSpec((1,depth,blk),lambda j:(j//per,0,j%per)),out],
        out_specs=out,out_shape=jax.ShapeDtypeStruct((rows,parts*cols),BF),compiler_params=params(),
        cost_estimate=TINY,name="hidden_slope")(g,w,s)

def hidden_down_kernel(a_ref, w_ref, y_ref):
    cols=w_ref.shape[2]
    total=dot(a_ref[:,0:cols],w_ref[0],NT)
    for z in range(1,w_ref.shape[0]):
        total=total+dot(a_ref[:,z*cols:(z+1)*cols],w_ref[z],NT)
    y_ref[...]=total.astype(y_ref.dtype)

def hidden_down(a,w,half,kind):
    rows=a.shape[0]//2; parts,depth,cols=w.shape; blk=256
    return pl.pallas_call(hidden_down_kernel,grid=(depth//blk,),
        in_specs=[pl.BlockSpec((rows,parts*cols),lambda j:(half,0)),pl.BlockSpec((parts,blk,cols),lambda j:(0,j,0))],
        out_specs=pl.BlockSpec((rows,blk),lambda j:(0,j)),out_shape=jax.ShapeDtypeStruct((rows,depth),kind),compiler_params=params(),
        cost_estimate=TINY,name="hidden_down")(a,w)


from jax.sharding import PartitionSpec as P

STEP=10
NORM_EPSILON = 1e-05
BETA_FIRST = 0.9
BETA_SECOND = 0.95
LEARN_RATE = 0.1
GAIN_RATE = 0.5
WEIGHT_DECAY = 0.1
ADAM_EPSILON = 1e-08
CLIP_LIMIT = 1.0
GELU_SCALE = 0.7978845608028654
GELU_CUBIC = 0.044715

PAIR = [(0, 1), (1, 0), (2, 3), (3, 2)]
MIDDLE = [(1, 2), (2, 1)]
OUTWARD = [(1, 0), (2, 3)]
INWARD = [(0, 1), (3, 2)]
ACROSS = [(0, 2), (1, 3), (2, 0), (3, 1)]


def tie(*values):
    return lax.optimization_barrier(values)


def swap_dp(value, size, bit):
    return lax.ppermute(value, "dp", [(i, i ^ bit) for i in range(size)])


def move_mp(value, pairs):
    return lax.ppermute(value, "mp", pairs)


def adam_update(master, gradient, momentum, variance, factor, rate, decay_rate):
    clipped = gradient * factor
    moment = BETA_FIRST * momentum + (1.0 - BETA_FIRST) * clipped
    square = BETA_SECOND * variance + (1.0 - BETA_SECOND) * clipped * clipped
    step_ratio = (
        moment
        / (1.0 - BETA_FIRST**STEP)
        / (jnp.sqrt(square / (1.0 - BETA_SECOND**STEP)) + ADAM_EPSILON)
    )
    return (master - rate * (step_ratio + decay_rate * master), moment, square)


def norm_parts(values):
    center = values - jnp.mean(values, axis=-1, keepdims=True)
    spread = jnp.mean(center * center, axis=-1, keepdims=True)
    scale = lax.rsqrt(spread + NORM_EPSILON)
    return center * scale, scale


def norm_back(values, grad, gain_row):
    unit, scale = norm_parts(values)
    scaled = grad * gain_row
    back = scale * (
        scaled
        - jnp.mean(scaled, axis=-1, keepdims=True)
        - unit * jnp.mean(scaled * unit, axis=-1, keepdims=True)
    )
    return back, jnp.sum(grad * unit, axis=0), jnp.sum(grad, axis=0)


def per_device(
    image_states, text_states, text_mask, cotangent,
    input_weights, output_weights, hidden_weights, norm_gains,
    input_momentum, output_momentum, hidden_momentum, gains_momentum,
    input_variance, output_variance, hidden_variance, gains_variance,
):
    size = lax.axis_size("dp")
    lines = lax.axis_size("mp")
    dp = lax.axis_index("dp")
    mp = lax.axis_index("mp")
    core = dp % 2
    chip = dp // 2
    chips = size // 2
    middle = (mp == 1) | (mp == 2)
    bits = []
    bit = 2
    while bit < size:
        bits.append(bit)
        bit *= 2
    width = image_states.shape[-1]
    block = width // chips
    part = width // size

    def pick(first, second):
        return jnp.where(core == 0, first, second)

    def swap_core(value):
        return swap_dp(value, size, 1)

    def reorder(value):
        return jnp.concatenate(
            [lax.dynamic_slice_in_dim(value, (chip ^ p) * block, block, value.ndim - 1) for p in range(chips)], -1
        )

    def own_half(stack):
        half = stack.shape[-1] // 2
        keep = lax.dynamic_slice_in_dim(stack, core * half, half, 2)
        send = lax.dynamic_slice_in_dim(stack, (1 - core) * half, half, 2)
        recv = swap_core(send)
        return jnp.concatenate([pick(keep, recv), pick(recv, keep)], 1)

    pairs = [bits[i : i + 2] for i in range(0, len(bits), 2)]

    near = pairs[0] if pairs else []

    def phase_low(low):
        return {b: swap_dp(low, size, b) for b in near}

    def phase_on(low, high, lows, highs):
        found = {0: (low, high)}
        for b in near:
            found[b] = (lows[b], highs[b])
        if len(near) == 2:
            a, b = near
            found[a ^ b] = (swap_dp(lows[b], size, a), swap_dp(highs[a], size, b))
        for bit in bits[2:]:
            for c in sorted(found):
                found[c ^ bit] = tuple(swap_dp(v, size, bit) for v in found[c])
        return found

    def whole_on(line, wholes):
        found = {0: (line,)}
        for b in near:
            found[b] = (wholes[b],)
        if len(near) == 2:
            a, b = near
            low, high = split_halves(wholes[b], wholes[a])
            found[a ^ b] = (swap_dp(low, size, a), swap_dp(high, size, b))
        for bit in bits[2:]:
            for c in sorted(found):
                found[c ^ bit] = tuple(swap_dp(v, size, bit) for v in found[c])
        return found

    def assemble(found):
        return place_pieces([found[2 * p] for p in range(chips)], 2 * part)

    def assemble_gains(found):
        per = norm_gains.shape[1]
        count = 2 * 2 * 6 * per
        rows = []
        for p in range(chips):
            pieces = [v[z, 0, 2 * part :].reshape(-1)[:count] for v in found[2 * p] for z in range(v.shape[0])]
            rows.append(jnp.stack(pieces, 0).reshape(lines, 2, 2, 6, per).astype(F32))
        stacked = jnp.stack(rows, 0)
        stacked = jnp.stack(
            [lax.dynamic_index_in_dim(stacked, (z - mp) % lines, 1, keepdims=False) for z in range(lines)], 2
        )
        total = stacked[:, :, :, 0] + stacked[:, :, :, 1]
        return total.transpose(3, 0, 1, 2, 4).reshape(6, width)

    def slices(grad):
        half = grad.shape[-1] // 2
        found = {}
        for p in range(chips):
            rows = lax.slice_in_dim(grad, p * 2 * part, (p + 1) * 2 * part, axis=1)
            found[2 * p] = (rows[..., :half], rows[..., half:])
        for bit in reversed(bits[2:]):
            found = {
                c: tuple(u + swap_dp(v, size, bit) for u, v in zip(found[c], found[c ^ bit])) for c in found if not c & bit
            }
        return found

    def back_far(found):
        if len(near) < 2:
            return {}
        a, b = near
        return {"low": swap_dp(found[a ^ b][0], size, a), "high": swap_dp(found[a ^ b][1], size, b)}

    def back_plain(found):
        if len(near) < 2:
            return {}
        a, b = near
        return {"low": swap_dp(found[a][0], size, a), "high": swap_dp(found[b][1], size, b)}

    def back_summed(found, far):
        if not near:
            return {}
        if len(near) < 2:
            return {"low": swap_dp(found[near[0]][0], size, near[0]), "high": swap_dp(found[near[0]][1], size, near[0])}
        a, b = near
        return {
            "low": swap_dp(found[b][0] + far["low"], size, b),
            "high": swap_dp(found[a][1] + far["high"], size, a),
        }

    def back_total(found, plain, summed):
        low, high = found[0]
        for got in (plain, summed):
            if got:
                low, high = low + got["low"], high + got["high"]
        return jnp.concatenate([low, high], -1)

    def lay(total):
        quarter = total.shape[-1] // lines
        return [total[..., z * quarter : (z + 1) * quarter] for z in range(lines)]

    def lay_hidden(total):
        group = 128 * lines
        count = total.shape[-1] // group
        return [
            jnp.concatenate([total[..., j * group + z * 128 : j * group + (z + 1) * 128] for j in range(count)], -1)
            for z in range(lines)
        ]

    def scatter_line(pieces):
        return lax.psum_scatter(jnp.stack(pieces, 0), "mp", scatter_dimension=0, tiled=True)[0]

    def scatter_shift(pieces):
        total = pieces[0].astype(F32)
        for k in range(1, lines):
            total = total + move_mp(pieces[k], [(i, (i + k) % lines) for i in range(lines)]).astype(F32)
        return total.astype(BF)

    def scatter_core(mine):
        keep = pick(mine[:, :part], mine[:, part:])
        recv = swap_core(pick(mine[:, part:], mine[:, :part]))
        return jnp.concatenate([pick(keep, recv), pick(recv, keep)], -1).astype(F32)

    items = image_states.shape[0]
    run = image_states.shape[1] // 2

    def bring_core(value):
        blocks = value.reshape(items, 2, run, width)
        keep = pick(blocks[:, 0], blocks[:, 1])
        recv = swap_core(pick(blocks[:, 1], blocks[:, 0]))
        return jnp.concatenate([pick(keep, recv), pick(recv, keep)], 0)

    def bring_line(whole):
        return lax.all_to_all(whole, "mp", 0, 0, tiled=True)

    def bring_last(whole):
        return reorder(whole.reshape(lines * run, width))

    def give_line(value, rows):
        return lax.all_to_all(reorder(value).reshape(lines, rows, width), "mp", 0, 0, tiled=True)

    def give_core(whole):
        low, high = whole[:items], whole[items:]
        keep = pick(low, high)
        recv = swap_core(pick(high, low))
        rows = whole.shape[1]
        return jnp.stack([pick(keep, recv), pick(recv, keep)], 1).reshape(items, 2 * rows, width).astype(F32)

    def both(value):
        return jnp.concatenate([value, swap_core(value)], 0)

    def joined(left, right, dims):
        half = left.shape[0] // 2
        other = dot(left[half:], right, dims).astype(BF)
        return dot(left[:half], right, dims) + swap_core(other).astype(F32)

    def sum_all(value):
        bit = 1
        while bit < size:
            value = value + swap_dp(value, size, bit)
            bit *= 2
        value = value + move_mp(value, PAIR)
        return value + move_mp(value, ACROSS)

    def sum_fast(value):
        value = value + swap_core(value)
        for i in range(0, len(bits), 2):
            pair = bits[i : i + 2]
            others = pair + [sum(pair)] if len(pair) == 2 else pair
            value = value + sum(swap_dp(value, size, b) for b in others)
        shifts = [[(i, (i + k) % lines) for i in range(lines)] for k in range(1, lines)]
        return value + sum(move_mp(value, pairs) for pairs in shifts)

    low = jnp.concatenate([input_weights[:3], output_weights[:1], input_weights[3:], output_weights[1:]], 0).astype(BF)
    own_inout = own_half(low)
    own_hidden = own_half(hidden_weights.astype(BF))
    blocks = own_hidden.shape[-1] // 128

    def in_blocks(shard):
        return jnp.stack([shard[:, j * 128 : (j + 1) * 128] for j in range(blocks)], 0)

    rest = jnp.concatenate([own_inout[4:], in_blocks(own_hidden[0]), in_blocks(own_hidden[1])], 0)

    gains_high = norm_gains.astype(BF)
    gains_low = (norm_gains - gains_high.astype(F32)).astype(BF)
    gains_own = jnp.stack([gains_high, gains_low], 0)
    gains_recv = swap_core(gains_own)
    gains_chip = jnp.stack([pick(gains_own, gains_recv), pick(gains_recv, gains_own)], 0)
    extra = -(-gains_chip.size // 1024) * 8
    gains_rows = jnp.pad(gains_chip.reshape(-1), (0, extra * 128 - gains_chip.size)).reshape(1, extra, 128)
    gains_rows = jnp.pad(gains_rows, ((0, 3), (0, 0), (0, 0)))
    own_self = jnp.concatenate([own_inout[:4], gains_rows], 1)

    def shift(value, step):
        return move_mp(value, [(i, (i - step) % lines) for i in range(lines)])

    moved = [own_self] + [shift(own_self, k) for k in range(1, lines)]
    image_core = bring_core(image_states)
    mid = lines // 2
    moved, image_core, rest = tie(moved, image_core, rest)
    self_line = jnp.stack(moved, 0)
    self_whole = phase_low(self_line)
    image_line = bring_line(image_core)
    self_whole, rest, image_line = tie(self_whole, rest, image_line)
    line_cross = lax.all_gather(rest[:4], "mp", axis=0)
    found_self = whole_on(self_line, self_whole)
    image_all = both(bring_last(image_line))
    line_cross, rest_hidden = tie(line_cross, rest[4:])
    line_hidden = lax.all_gather(rest_hidden, "mp", axis=0)
    cot_core = bring_core(cotangent)
    line_hidden, cot_core = tie(line_hidden, cot_core)

    which = mp % items
    mine = lax.dynamic_index_in_dim(text_states, which, 0, keepdims=False)
    mine_mask = lax.dynamic_index_in_dim(text_mask, which, 0, keepdims=False).astype(F32)
    here = (mp // items) == core
    text = reorder(jnp.where(here, mine, swap_core(mine)))
    valid = jnp.where(here, mine_mask, swap_core(mine_mask))
    valid = jnp.broadcast_to(valid[:, None], (valid.shape[0], 128))

    core_index = core.astype(jnp.int32).reshape(1)

    half = image_all.shape[0] // 2
    found_self, image_all = tie(found_self, image_all)
    weights_self = assemble(found_self)
    gain_rows = assemble_gains(found_self)
    cross_low, cross_high = line_cross[:mid], line_cross[mid:]
    cross_lows = phase_low(cross_low)
    image_float = image_all.astype(F32)
    image_own = image_float[:half]
    unit, _ = norm_parts(image_float)
    h1 = (unit * gain_rows[0] + gain_rows[1]).astype(BF)
    q1, k1, v1 = (dot(h1, weights_self[j], NN).astype(BF) for j in range(3))
    q1, k1, v1, cross_lows = tie(q1, k1, v1, cross_lows)
    cross_highs = phase_low(cross_high)
    o1, l1 = self_fwd(core_index, q1, k1, v1)
    o1, cross_lows, cross_highs, line_hidden = tie(o1, cross_lows, cross_highs, line_hidden)
    found_cross = phase_on(cross_low, cross_high, cross_lows, cross_highs)
    up_low, up_high = line_hidden[:mid, :blocks], line_hidden[mid:, :blocks]
    down_low, down_high = line_hidden[:mid, blocks:], line_hidden[mid:, blocks:]
    up_lows = phase_low(up_low)
    r1 = image_own + joined(o1, weights_self[3], NT)
    unit, _ = norm_parts(r1)
    h2 = both((unit * gain_rows[2] + gain_rows[3]).astype(BF))
    h2, found_cross, up_lows = tie(h2, found_cross, up_lows)
    weights_cross = assemble(found_cross)
    up_highs = phase_low(up_high)
    q2 = dot(h2, weights_cross[0], NN).astype(BF)
    k2, v2 = (dot(text, weights_cross[j], NN).astype(BF) for j in (1, 2))
    o2, l2 = cross_fwd(valid, q2, k2, v2)
    o2, up_lows, up_highs = tie(o2, up_lows, up_highs)
    found_up = phase_on(up_low, up_high, up_lows, up_highs)
    down_lows = phase_low(down_low)
    cot_line = bring_line(cot_core)
    r2 = r1 + joined(o2, weights_cross[3], NT)
    unit, _ = norm_parts(r2)
    h3 = both((unit * gain_rows[4] + gain_rows[5]).astype(BF))
    h3, found_up, down_lows = tie(h3, found_up, down_lows)
    weights_up = assemble(found_up)
    down_highs = phase_low(down_high)
    e, slope = hidden_up(h3, weights_up)
    e, down_lows, down_highs, cot_line = tie(e, down_lows, down_highs, cot_line)
    found_down = phase_on(down_low, down_high, down_lows, down_highs)
    cot_own = bring_last(cot_line)
    cot = both(cot_own)
    cot_float = cot_own.astype(F32)
    grad_down = dot(cot, e, TN).astype(BF)
    e, slope, found_down, grad_down = tie(e, slope, found_down, grad_down)
    weights_down = assemble(found_down)

    def joined_hidden(value, weights):
        other = hidden_down(value, weights, 1, BF)
        return hidden_down(value, weights, 0, F32) + swap_core(other).astype(F32)

    send_down = slices(grad_down[None])
    far_down = back_far(send_down)
    du = hidden_slope(cot, weights_down, slope)
    du, far_down = tie(du, far_down)
    plain_down = back_plain(send_down)
    grad_up = dot(h3, du, TN).astype(BF)
    grad_up, far_down, plain_down = tie(grad_up, far_down, plain_down)
    summed_down = back_summed(send_down, far_down)
    send_up = slices(grad_up[None])
    far_up = back_far(send_up)
    dh3 = joined_hidden(du, weights_up)
    back, gain_five, shift_six = norm_back(r2, dh3, gain_rows[4])
    dr2 = cot_float + back
    z2 = both(dr2.astype(BF))
    z2, summed_down, far_up = tie(z2, summed_down, far_up)
    plain_up = back_plain(send_up)
    near_down = scatter_line(lay_hidden(back_total(send_down, plain_down, summed_down)))
    layer_own = r2 + joined_hidden(e, weights_down)
    do2 = dot(z2, weights_cross[3], NN).astype(BF)
    go1 = dot(z2, o2, TN).astype(BF)
    dq2, dk2, dv2 = cross_bwd(valid, q2, k2, v2, do2, l2)
    dq2, dk2, dv2, plain_up, far_up, layer_own = tie(dq2, dk2, dv2, plain_up, far_up, layer_own)
    layer_line = give_line(layer_own.astype(BF), run)
    summed_up = back_summed(send_up, far_up)
    dh2 = joined(dq2, weights_cross[0], NT)
    gi3 = dot(h2, dq2, TN).astype(BF)
    gi4 = dot(text, dk2, TN).astype(BF)
    gi5 = dot(text, dv2, TN).astype(BF)
    back, gain_three, shift_four = norm_back(r1, dh2, gain_rows[2])
    dr1 = dr2 + back
    z1 = both(dr1.astype(BF))
    z1, summed_up, gi3, gi4, gi5, go1 = tie(z1, summed_up, gi3, gi4, gi5, go1)
    send_cross = slices(jnp.stack([gi3, gi4, gi5, go1]))
    far_cross = back_far(send_cross)
    near_up = scatter_line(lay_hidden(back_total(send_up, plain_up, summed_up)))
    text_part = dot(dk2, weights_cross[1], NT) + dot(dv2, weights_cross[2], NT)
    share = text.shape[0] // (2 * lines)
    text_part = text_part.reshape(lines, 2, share, width)
    text_own = pick(text_part[:, 0], text_part[:, 1]) + swap_core(
        pick(text_part[:, 1], text_part[:, 0]).astype(BF)
    ).astype(F32)
    text_line = give_line(text_own.astype(BF).reshape(lines * share, width), share)
    do1 = dot(z1, weights_self[3], NN).astype(BF)
    go0 = dot(z1, o1, TN).astype(BF)
    do1, go0, far_cross, layer_line = tie(do1, go0, far_cross, layer_line)
    plain_cross = back_plain(send_cross)
    summed_cross = back_summed(send_cross, far_cross)
    dq1, dk1, dv1 = self_bwd(core_index, q1, k1, v1, do1, l1)
    dq1, dk1, dv1, plain_cross, summed_cross, text_line = tie(dq1, dk1, dv1, plain_cross, summed_cross, text_line)
    gi0, gi1, gi2 = (dot(h1, g, TN).astype(BF) for g in (dq1, dk1, dv1))
    grad_self = jnp.stack([gi0, gi1, gi2, go0])
    send_self = slices(grad_self)
    far_self = back_far(send_self)
    plain_self = back_plain(send_self)
    send_self, dq1, dk1, dv1, plain_cross, summed_cross, near_up, near_down = tie(
        send_self, dq1, dk1, dv1, plain_cross, summed_cross, near_up, near_down
    )
    near_cross = scatter_line(lay(back_total(send_cross, plain_cross, summed_cross)))

    def three(at):
        return (
            dot(dq1[at], weights_self[0], NT) + dot(dk1[at], weights_self[1], NT) + dot(dv1[at], weights_self[2], NT)
        )

    dh1 = three(slice(0, half)) + swap_core(three(slice(half, None)).astype(BF)).astype(F32)
    dh1, far_self, plain_self = tie(dh1, far_self, plain_self)
    summed_self = back_summed(send_self, far_self)
    back, gain_one, shift_two = norm_back(image_own, dh1, gain_rows[0])
    image_own_grad = (dr1 + back).astype(BF)
    gains_total = reorder(jnp.stack([gain_one, shift_two, gain_three, shift_four, gain_five, shift_six]))
    image_line = give_line(image_own_grad, run)
    summed_self, gains_total = tie(summed_self, gains_total)
    gains_total = sum_all(gains_total)
    near_self = scatter_shift(lay(back_total(send_self, plain_self, summed_self)))
    near_self, image_line, near_cross, near_up, near_down = tie(near_self, image_line, near_cross, near_up, near_down)
    shard_down = scatter_core(near_down)
    shard_up = scatter_core(near_up)
    shard_cross = scatter_core(near_cross)
    shard_self = scatter_core(near_self)
    layer_out = give_core(layer_line)
    image_gradient = give_core(image_line)
    text_gradient = give_core(text_line)
    gains_shard = lax.dynamic_slice_in_dim(
        gains_total, (dp * lines + mp) * norm_gains.shape[1], norm_gains.shape[1], 1
    )

    input_shard = jnp.concatenate([shard_self[:3], shard_cross[:3]], 0)
    output_shard = jnp.concatenate([shard_self[3:], shard_cross[3:]], 0)
    hidden_shard = jnp.concatenate([shard_up, shard_down], 0)
    square_total = jnp.sum(input_shard * input_shard) + jnp.sum(output_shard * output_shard)
    square_total = square_total + jnp.sum(hidden_shard * hidden_shard) + jnp.sum(gains_shard * gains_shard)
    global_norm = jnp.sqrt(sum_fast(jnp.full((8, 128), square_total)))[0, 0]
    factor = jnp.minimum(1.0, CLIP_LIMIT / (global_norm + 1e-06))
    input_updated, input_moment, input_square = adam_update(
        input_weights, input_shard, input_momentum, input_variance, factor, LEARN_RATE, WEIGHT_DECAY
    )
    output_updated, output_moment, output_square = adam_update(
        output_weights, output_shard, output_momentum, output_variance, factor, LEARN_RATE, WEIGHT_DECAY
    )
    hidden_updated, hidden_moment, hidden_square = adam_update(
        hidden_weights, hidden_shard, hidden_momentum, hidden_variance, factor, LEARN_RATE, WEIGHT_DECAY
    )
    gains_updated, gains_moment, gains_square = adam_update(
        norm_gains, gains_shard, gains_momentum, gains_variance, factor, GAIN_RATE, 0.0
    )
    return (
        layer_out, image_gradient, text_gradient, global_norm,
        input_updated, output_updated, hidden_updated, gains_updated,
        input_moment, output_moment, hidden_moment, gains_moment,
        input_square, output_square, hidden_square, gains_square,
    )


def solution(mesh):
    rows, weight, gains = P("dp", "mp", None), P(None, "dp", "mp"), P(None, ("dp", "mp"))
    return jax.shard_map(
        per_device,
        mesh=mesh,
        in_specs=(rows, P("dp", None, None), P("dp", None), rows) + (weight, weight, weight, gains) * 3,
        out_specs=(rows, rows, rows, P()) + (weight, weight, weight, gains) * 3,
        check_vma=False,
    )
```

```python
import math
import jax, jax.numpy as jnp
from jax import lax
from jax.experimental import pallas as pl
from jax.experimental.pallas import tpu as pltpu
BF=jnp.bfloat16; F32=jnp.float32
HEAD_DIM=64; MASKED=-1e30; BQ=256
NT=(((1,),(1,)),((),())); NN=(((1,),(0,)),((),())); TN=(((0,),(0,)),((),()))
TINY=pl.CostEstimate(flops=1,bytes_accessed=1,transcendentals=0)
def dot(a,b,dims): return lax.dot_general(a,b,dims,preferred_element_type=F32)

def place_of(block, core, half):
    return pl.multiple_of(((block % 2) ^ core) * half + (block // 2) * 128, 128)

def self_fwd_kernel(core_ref, q_ref, k_ref, v_ref, o_ref, l_ref, qs, ks, vs, *, seq):
    core=core_ref[0]; half=seq//2
    for b in range(seq//128):
        at=pl.ds(place_of(b,core,half),128); to=slice(b*128,b*128+128)
        qs[to,:]=(q_ref[at,:].astype(F32)*0.125).astype(BF)
        ks[to,:]=k_ref[at,:]
        vs[to,:]=v_ref[at,:]
    low=lax.broadcasted_iota(jnp.int32,(1,128),1)<HEAD_DIM
    for i in range(seq//BQ):
        n=(i+1)*BQ
        q=qs[i*BQ:n,:]
        outs=[]
        for h in range(2):
            keep=low if h==0 else ~low
            kh=jnp.where(keep,ks[0:n,:],jnp.zeros((),BF))
            s=dot(kh,q,NT)
            tri=lax.broadcasted_iota(jnp.int32,(BQ,BQ),0)<=lax.broadcasted_iota(jnp.int32,(BQ,BQ),1)
            diag=jnp.where(tri,s[n-BQ:,:],MASKED)
            s=diag if n==BQ else jnp.concatenate([s[:n-BQ],diag],0)
            m=jnp.max(s,axis=0,keepdims=True)
            e=jnp.exp(s-m)
            t=jnp.sum(e,axis=0,keepdims=True)
            l_ref[0,h:h+1,i*BQ:n]=m+jnp.log(t)
            vh=vs[0:n,h*64:h*64+64]
            o=dot(vh,e.astype(BF),TN)
            outs.append(o*(1.0/t))
        o=jnp.concatenate(outs,0).T.astype(BF)
        for j in range(BQ//128):
            o_ref[pl.ds(place_of(i*(BQ//128)+j,core,half),128),:]=o[j*128:j*128+128]

def self_bwd_kernel(core_ref, q_ref, k_ref, v_ref, g_ref, l_ref, dq_ref, dk_ref, dv_ref, qs, ks, vs, gs, dka, dva, *, seq):
    core=core_ref[0]; half=seq//2
    for b in range(seq//128):
        at=pl.ds(place_of(b,core,half),128); to=slice(b*128,b*128+128)
        qs[to,:]=(q_ref[at,:].astype(F32)*0.125).astype(BF)
        ks[to,:]=k_ref[at,:]
        vs[to,:]=v_ref[at,:]
        gs[to,:]=g_ref[at,:]
    dka[...]=jnp.zeros_like(dka); dva[...]=jnp.zeros_like(dva)
    low=lax.broadcasted_iota(jnp.int32,(1,128),1)<HEAD_DIM
    zero=jnp.zeros((),BF)
    for i in range(seq//BQ):
        n=(i+1)*BQ; rows=slice(i*BQ,n)
        q=qs[rows,:]; g=gs[rows,:]
        ps=[]; dss=[]
        for h in range(2):
            keep=low if h==0 else ~low
            kh=jnp.where(keep,ks[0:n,:],zero)
            vh=jnp.where(keep,vs[0:n,:],zero)
            s=dot(kh,q,NT)
            tri=lax.broadcasted_iota(jnp.int32,(BQ,BQ),0)<=lax.broadcasted_iota(jnp.int32,(BQ,BQ),1)
            diag=jnp.where(tri,s[n-BQ:,:],MASKED)
            s=diag if n==BQ else jnp.concatenate([s[:n-BQ],diag],0)
            p=jnp.exp(s-l_ref[0,h:h+1,rows])
            dp=dot(vh,g,NT)
            delta=jnp.sum(p*dp,axis=0,keepdims=True)
            ds=(p*(dp-delta)).astype(BF)
            ps.append(p.astype(BF)); dss.append(ds)
        qa=jnp.concatenate([jnp.where(low,q,zero),jnp.where(low,zero,q)],0)
        ga=jnp.concatenate([jnp.where(low,g,zero),jnp.where(low,zero,g)],0)
        dva[0:n,:]+=dot(jnp.concatenate(ps,1),ga,NN)
        dka[0:n,:]+=dot(jnp.concatenate(dss,1),qa,NN)
        k=ks[0:n,:]
        dqt=jnp.concatenate([dot(ks[0:n,0:64],dss[0],TN),dot(ks[0:n,64:128],dss[1],TN)],0)
        dq=(dqt.T*0.125).astype(BF)
        for j in range(BQ//128):
            dq_ref[pl.ds(place_of(i*(BQ//128)+j,core,half),128),:]=dq[j*128:j*128+128]
    for b in range(seq//128):
        at=pl.ds(place_of(b,core,half),128)
        dk_ref[at,:]=dka[b*128:b*128+128,:].astype(BF)
        dv_ref[at,:]=dva[b*128:b*128+128,:].astype(BF)

def cross_fwd_kernel(mask_ref, q_ref, k_ref, v_ref, o_ref, l_ref, *, seq):
    low=lax.broadcasted_iota(jnp.int32,(1,128),1)<HEAD_DIM
    zero=jnp.zeros((),BF)
    valid=mask_ref[:,0:1]>0
    k=k_ref[...]; v=v_ref[...]
    for i in range(seq//BQ):
        rows=slice(i*BQ,(i+1)*BQ)
        q=(q_ref[rows,:].astype(F32)*0.125).astype(BF)
        outs=[]
        for h in range(2):
            kh=jnp.where(low if h==0 else ~low,k,zero)
            s=jnp.where(valid,dot(kh,q,NT),MASKED)
            m=jnp.max(s,axis=0,keepdims=True)
            e=jnp.exp(s-m)
            t=jnp.sum(e,axis=0,keepdims=True)
            l_ref[0,h:h+1,rows]=m+jnp.log(t)
            outs.append(dot(v[:,h*64:h*64+64],e.astype(BF),TN)*(1.0/t))
        o_ref[rows,:]=jnp.concatenate(outs,0).T.astype(BF)

def cross_bwd_kernel(mask_ref, q_ref, k_ref, v_ref, g_ref, l_ref, dq_ref, dk_ref, dv_ref, *, seq):
    low=lax.broadcasted_iota(jnp.int32,(1,128),1)<HEAD_DIM
    zero=jnp.zeros((),BF)
    valid=mask_ref[:,0:1]>0
    k=k_ref[...]; v=v_ref[...]
    dk=jnp.zeros(k.shape,F32); dv=jnp.zeros(k.shape,F32)
    for i in range(seq//BQ):
        rows=slice(i*BQ,(i+1)*BQ)
        q=(q_ref[rows,:].astype(F32)*0.125).astype(BF); g=g_ref[rows,:]
        ps=[]; dss=[]; dqs=[]
        for h in range(2):
            keep=low if h==0 else ~low
            kh=jnp.where(keep,k,zero); vh=jnp.where(keep,v,zero)
            s=jnp.where(valid,dot(kh,q,NT),MASKED)
            p=jnp.exp(s-l_ref[0,h:h+1,rows])
            dp=dot(vh,g,NT)
            delta=jnp.sum(p*dp,axis=0,keepdims=True)
            ds=(p*(dp-delta)).astype(BF)
            ps.append(p.astype(BF)); dss.append(ds)
            dqs.append(dot(k[:,h*64:h*64+64],ds,TN))
        qa=jnp.concatenate([jnp.where(low,q,zero),jnp.where(low,zero,q)],0)
        ga=jnp.concatenate([jnp.where(low,g,zero),jnp.where(low,zero,g)],0)
        dv=dv+dot(jnp.concatenate(ps,1),ga,NN)
        dk=dk+dot(jnp.concatenate(dss,1),qa,NN)
        dq_ref[rows,:]=(jnp.concatenate(dqs,0).T*0.125).astype(BF)
    dk_ref[...]=dk.astype(BF); dv_ref[...]=dv.astype(BF)

def col(rows): return pl.BlockSpec((rows,128),lambda p,*_:(0,p))
LSPEC=pl.BlockSpec((1,2,None),lambda p,*_:(p,0,0))
def params(): return pltpu.CompilerParams(vmem_limit_bytes=48*1024*1024)
def self_fwd(core,q,k,v):
    seq,cols=q.shape; pairs=cols//128
    return pl.pallas_call(lambda *r: self_fwd_kernel(*r,seq=seq),
        grid_spec=pltpu.PrefetchScalarGridSpec(num_scalar_prefetch=1,grid=(pairs,),in_specs=[col(seq)]*3,
            out_specs=[col(seq),pl.BlockSpec((1,2,seq),lambda p,*_:(p,0,0))],scratch_shapes=[pltpu.VMEM((seq,128),BF)]*3),
        out_shape=[jax.ShapeDtypeStruct((seq,cols),BF),jax.ShapeDtypeStruct((pairs,2,seq),F32)],
        compiler_params=params(),
        cost_estimate=TINY,name="self_forward")(core,q,k,v)
def self_bwd(core,q,k,v,g,l):
    seq,cols=q.shape; pairs=cols//128
    return pl.pallas_call(lambda *r: self_bwd_kernel(*r,seq=seq),
        grid_spec=pltpu.PrefetchScalarGridSpec(num_scalar_prefetch=1,grid=(pairs,),in_specs=[col(seq)]*4+[pl.BlockSpec((1,2,seq),lambda p,*_:(p,0,0))],
            out_specs=[col(seq)]*3,scratch_shapes=[pltpu.VMEM((seq,128),BF)]*4+[pltpu.VMEM((seq,128),F32)]*2),
        out_shape=[jax.ShapeDtypeStruct((seq,cols),BF)]*3,
        compiler_params=params(),
        cost_estimate=TINY,name="self_backward")(core,q,k,v,g,l)
def cross_fwd(mask,q,k,v):
    seq,cols=q.shape; text=k.shape[0]; pairs=cols//128
    return pl.pallas_call(lambda *r: cross_fwd_kernel(*r,seq=seq),grid=(pairs,),
        in_specs=[pl.BlockSpec((text,128),lambda p:(0,0)),col(seq),col(text),col(text)],
        out_specs=[col(seq),pl.BlockSpec((1,2,seq),lambda p:(p,0,0))],
        out_shape=[jax.ShapeDtypeStruct((seq,cols),BF),jax.ShapeDtypeStruct((pairs,2,seq),F32)],
        compiler_params=params(),
        cost_estimate=TINY,name="cross_forward")(mask,q,k,v)
def cross_bwd(mask,q,k,v,g,l):
    seq,cols=q.shape; text=k.shape[0]; pairs=cols//128
    return pl.pallas_call(lambda *r: cross_bwd_kernel(*r,seq=seq),grid=(pairs,),
        in_specs=[pl.BlockSpec((text,128),lambda p:(0,0)),col(seq),col(text),col(text),col(seq),pl.BlockSpec((1,2,seq),lambda p:(p,0,0))],
        out_specs=[col(seq),col(text),col(text)],
        out_shape=[jax.ShapeDtypeStruct((seq,cols),BF),jax.ShapeDtypeStruct((text,cols),BF),jax.ShapeDtypeStruct((text,cols),BF)],
        compiler_params=params(),
        cost_estimate=TINY,name="cross_backward")(mask,q,k,v,g,l)

def split_halves(a,b):
    half,m,rows,cols=a.shape[0]//2,*a.shape[1:]
    def body(a_ref,b_ref,x_ref,y_ref):
        x_ref[...]=a_ref[...]
        y_ref[...]=b_ref[...]
    block=(half,1,rows,cols)
    out=jax.ShapeDtypeStruct((half,m,rows,cols),a.dtype)
    return pl.pallas_call(body,grid=(m,),
        in_specs=[pl.BlockSpec(block,lambda i:(0,i,0,0)),pl.BlockSpec(block,lambda i:(1,i,0,0))],
        out_specs=[pl.BlockSpec(block,lambda i:(0,i,0,0))]*2,out_shape=[out,out],compiler_params=params(),
        cost_estimate=TINY,name="split_halves")(a,b)

def place_pieces(groups,chip,rows):
    first=groups[0][0]
    _,m,_,cols=first.shape
    width=sum(v.shape[0] for v in groups[0])*cols
    flat=[v for g in groups for v in g]
    shapes=[[v.shape[0] for v in g] for g in groups]
    def body(chip_ref,*refs):
        ins,out=refs[:len(flat)],refs[len(flat)]
        at=0
        for p,s in enumerate(shapes):
            def fill(at=at,s=s):
                z=0
                for i,k in enumerate(s):
                    for j in range(k):
                        out[:,:,z*cols:(z+1)*cols]=ins[at+i][j,:,0:rows,:]; z+=1
            pl.when(pl.program_id(0)==p)(fill)
            at+=len(s)
    return pl.pallas_call(body,
        grid_spec=pltpu.PrefetchScalarGridSpec(num_scalar_prefetch=1,grid=(len(groups),),
            in_specs=[pl.BlockSpec(v.shape,lambda p,c:(0,0,0,0),pipeline_mode=pl.Buffered(1)) for v in flat],
            out_specs=pl.BlockSpec((m,rows,width),lambda p,c:(0,p^c[0],0))),
        out_shape=jax.ShapeDtypeStruct((m,rows*len(groups),width),first.dtype),compiler_params=params(),
        cost_estimate=TINY,name="place_pieces")(chip,*flat)

def hidden_up_kernel(h_ref, w_ref, e_ref, s_ref):
    w=w_ref[0]
    for i in range(h_ref.shape[0]//256):
        rows=slice(i*256,(i+1)*256)
        u=dot(h_ref[rows,:],w,NN)
        uu=u*u
        t=jnp.tanh(u*(0.7978845608028654+(0.7978845608028654*0.044715)*uu))
        p=0.5+0.5*t
        e_ref[rows,:]=(u*p).astype(BF)
        s_ref[rows,:]=(p+u*(p*(1.0-t))*(0.7978845608028654+(3.0*0.7978845608028654*0.044715)*uu)).astype(BF)

def hidden_up(h,w):
    rows,depth=h.shape; parts,_,cols=w.shape; blk=256; per=cols//blk
    out=pl.BlockSpec((rows,blk),lambda j:(0,j))
    return pl.pallas_call(hidden_up_kernel,grid=(parts*per,),
        in_specs=[pl.BlockSpec((rows,depth),lambda j:(0,0)),pl.BlockSpec((1,depth,blk),lambda j:(j//per,0,j%per))],
        out_specs=[out,out],out_shape=[jax.ShapeDtypeStruct((rows,parts*cols),BF)]*2,compiler_params=params(),
        cost_estimate=TINY,name="hidden_up")(h,w)

def hidden_slope_kernel(g_ref, w_ref, s_ref, d_ref):
    w=w_ref[0]
    for i in range(g_ref.shape[0]//256):
        rows=slice(i*256,(i+1)*256)
        d_ref[rows,:]=(dot(g_ref[rows,:],w,NN)*s_ref[rows,:].astype(F32)).astype(BF)

def hidden_slope(g,w,s):
    rows,depth=g.shape; parts,_,cols=w.shape; blk=256; per=cols//blk
    out=pl.BlockSpec((rows,blk),lambda j:(0,j))
    return pl.pallas_call(hidden_slope_kernel,grid=(parts*per,),
        in_specs=[pl.BlockSpec((rows,depth),lambda j:(0,0)),pl.BlockSpec((1,depth,blk),lambda j:(j//per,0,j%per)),out],
        out_specs=out,out_shape=jax.ShapeDtypeStruct((rows,parts*cols),BF),compiler_params=params(),
        cost_estimate=TINY,name="hidden_slope")(g,w,s)

def hidden_down_kernel(a_ref, w_ref, y_ref):
    cols=w_ref.shape[2]
    total=dot(a_ref[:,0:cols],w_ref[0],NT)
    for z in range(1,w_ref.shape[0]):
        total=total+dot(a_ref[:,z*cols:(z+1)*cols],w_ref[z],NT)
    y_ref[...]=total.astype(y_ref.dtype)

def hidden_down(a,w,half,kind):
    rows=a.shape[0]//2; parts,depth,cols=w.shape; blk=256
    return pl.pallas_call(hidden_down_kernel,grid=(depth//blk,),
        in_specs=[pl.BlockSpec((rows,parts*cols),lambda j:(half,0)),pl.BlockSpec((parts,blk,cols),lambda j:(0,j,0))],
        out_specs=pl.BlockSpec((rows,blk),lambda j:(0,j)),out_shape=jax.ShapeDtypeStruct((rows,depth),kind),compiler_params=params(),
        cost_estimate=TINY,name="hidden_down")(a,w)


def place_hidden(groups,chip,rows):
    first=groups[0][0]
    cols=first.shape[3]
    parts=sum(v.shape[0] for v in groups[0])
    flat=[v for g in groups for v in g]
    shapes=[[v.shape[0] for v in g] for g in groups]
    def body(chip_ref,*refs):
        ins,out=refs[:len(flat)],refs[len(flat)]
        at=0
        for p,s in enumerate(shapes):
            def fill(at=at,s=s):
                z=0
                for i,k in enumerate(s):
                    out[z:z+k]=ins[at+i][:,0]; z+=k
            pl.when(pl.program_id(0)==p)(fill)
            at+=len(s)
    return pl.pallas_call(body,
        grid_spec=pltpu.PrefetchScalarGridSpec(num_scalar_prefetch=1,grid=(len(groups),),
            in_specs=[pl.BlockSpec(v.shape,lambda p,c:(0,0,0,0),pipeline_mode=pl.Buffered(1)) for v in flat],
            out_specs=pl.BlockSpec((parts,rows,cols),lambda p,c:(0,p^c[0],0))),
        out_shape=jax.ShapeDtypeStruct((parts,rows*len(groups),cols),first.dtype),compiler_params=params(),
        cost_estimate=TINY,name="place_hidden")(chip,*flat)

def piece_grads(chip,lefts,rights,chips):
    tokens,depth=lefts[0].shape
    rows=depth//chips; m=len(rights); cols=rights[0][2]
    arrays=[]
    for _,v,_,_ in rights:
        if not any(v is w for w in arrays): arrays.append(v)
    where=[next(i for i,w in enumerate(arrays) if w is v) for _,v,_,_ in rights]
    nl,na=len(lefts),len(arrays)
    def body(chip_ref,*refs):
        ls,rs,outs=refs[:nl],refs[nl:nl+na],refs[nl+na:]
        turned=[l[...].T for l in ls]
        got=[]
        for j,(left,_,_,at) in enumerate(rights):
            r=rs[where[j]][:,at*cols:(at+1)*cols]
            got.append(dot(turned[left],r,NN).astype(BF))
        for p in range(chips):
            def fill(p=p):
                for j in range(m): outs[p][j]=got[j]
            pl.when(pl.program_id(0)==p)(fill)
    shape=jax.ShapeDtypeStruct((m,rows,cols),BF)
    return pl.pallas_call(body,
        grid_spec=pltpu.PrefetchScalarGridSpec(num_scalar_prefetch=1,grid=(chips,),
            in_specs=[pl.BlockSpec((tokens,rows),lambda p,c:(0,p^c[0])) for _ in lefts]
                +[pl.BlockSpec(v.shape,lambda p,c:(0,0),pipeline_mode=pl.Buffered(1)) for v in arrays],
            out_specs=[pl.BlockSpec((m,rows,cols),lambda p,c:(0,0,0))]*chips),
        out_shape=[shape]*chips,compiler_params=params(),cost_estimate=TINY,name="piece_grads")(chip,*lefts,*arrays)

def token_grad(a,b,parts):
    rows,depth=a.shape; cols=b.shape[1]//parts; blk=256
    def body(a_ref,b_ref,g_ref):
        turned=a_ref[...].T
        for z in range(parts):
            g_ref[z]=dot(turned,b_ref[:,z*cols:(z+1)*cols],NN).astype(BF)
    return pl.pallas_call(body,grid=(depth//blk,),
        in_specs=[pl.BlockSpec((rows,blk),lambda j:(0,j)),pl.BlockSpec(b.shape,lambda j:(0,0),pipeline_mode=pl.Buffered(1))],
        out_specs=pl.BlockSpec((parts,blk,cols),lambda j:(0,j,0)),out_shape=jax.ShapeDtypeStruct((parts,depth,cols),BF),compiler_params=params(),
        cost_estimate=TINY,name="token_grad")(a,b)


from jax.sharding import PartitionSpec as P

STEP=10
NORM_EPSILON = 1e-05
BETA_FIRST = 0.9
BETA_SECOND = 0.95
LEARN_RATE = 0.1
GAIN_RATE = 0.5
WEIGHT_DECAY = 0.1
ADAM_EPSILON = 1e-08
CLIP_LIMIT = 1.0
GELU_SCALE = 0.7978845608028654
GELU_CUBIC = 0.044715

PAIR = [(0, 1), (1, 0), (2, 3), (3, 2)]
MIDDLE = [(1, 2), (2, 1)]
OUTWARD = [(1, 0), (2, 3)]
INWARD = [(0, 1), (3, 2)]
ACROSS = [(0, 2), (1, 3), (2, 0), (3, 1)]


def tie(*values):
    return lax.optimization_barrier(values)


def swap_dp(value, size, bit):
    return lax.ppermute(value, "dp", [(i, i ^ bit) for i in range(size)])


def move_mp(value, pairs):
    return lax.ppermute(value, "mp", pairs)


def adam_update(master, gradient, momentum, variance, factor, rate, decay_rate):
    clipped = gradient * factor
    moment = BETA_FIRST * momentum + (1.0 - BETA_FIRST) * clipped
    square = BETA_SECOND * variance + (1.0 - BETA_SECOND) * clipped * clipped
    step_ratio = (
        moment
        / (1.0 - BETA_FIRST**STEP)
        / (jnp.sqrt(square / (1.0 - BETA_SECOND**STEP)) + ADAM_EPSILON)
    )
    return (master - rate * (step_ratio + decay_rate * master), moment, square)


def norm_parts(values):
    center = values - jnp.mean(values, axis=-1, keepdims=True)
    spread = jnp.mean(center * center, axis=-1, keepdims=True)
    scale = lax.rsqrt(spread + NORM_EPSILON)
    return center * scale, scale


def norm_back(values, grad, gain_row):
    unit, scale = norm_parts(values)
    scaled = grad * gain_row
    back = scale * (
        scaled
        - jnp.mean(scaled, axis=-1, keepdims=True)
        - unit * jnp.mean(scaled * unit, axis=-1, keepdims=True)
    )
    return back, jnp.sum(grad * unit, axis=0), jnp.sum(grad, axis=0)


def per_device(
    image_states, text_states, text_mask, cotangent,
    input_weights, output_weights, hidden_weights, norm_gains,
    input_momentum, output_momentum, hidden_momentum, gains_momentum,
    input_variance, output_variance, hidden_variance, gains_variance,
):
    size = lax.axis_size("dp")
    lines = lax.axis_size("mp")
    dp = lax.axis_index("dp")
    mp = lax.axis_index("mp")
    core = dp % 2
    chip = dp // 2
    chips = size // 2
    middle = (mp == 1) | (mp == 2)
    bits = []
    bit = 2
    while bit < size:
        bits.append(bit)
        bit *= 2
    width = image_states.shape[-1]
    block = width // chips
    part = width // size

    def pick(first, second):
        return jnp.where(core == 0, first, second)

    def swap_core(value):
        return swap_dp(value, size, 1)

    chip_index = chip.astype(jnp.int32).reshape(1)
    groups = [[d * lines + m for m in range(lines) for d in range(c, size, 2)] for c in range(2)]

    def own_half(stack):
        half = stack.shape[-1] // 2
        keep = lax.dynamic_slice_in_dim(stack, core * half, half, 2)
        send = lax.dynamic_slice_in_dim(stack, (1 - core) * half, half, 2)
        recv = swap_core(send)
        return jnp.concatenate([pick(keep, recv), pick(recv, keep)], 1)

    pairs = [bits[i : i + 2] for i in range(0, len(bits), 2)]

    near = pairs[0] if pairs else []

    def phase_first(line):
        return {b: swap_dp(line, size, b) for b in near}

    def whole_on(line, wholes):
        found = {0: (line,)}
        for b in near:
            found[b] = (wholes[b],)
        if len(near) == 2:
            a, b = near
            low, high = split_halves(wholes[b], wholes[a])
            found[a ^ b] = (swap_dp(low, size, a), swap_dp(high, size, b))
        for bit in bits[2:]:
            for c in sorted(found):
                found[c ^ bit] = tuple(swap_dp(v, size, bit) for v in found[c])
        return found

    def gather_column(own):
        found = {0: own}
        if len(near) == 2:
            a, b = near
            found[a], found[b] = swap_dp(own, size, a), swap_dp(own, size, b)
            found[a ^ b] = jnp.concatenate([swap_dp(found[b][:part], size, a), swap_dp(found[a][part:], size, b)], 0)
        else:
            for a in near:
                found[a] = swap_dp(own, size, a)
        for bit in bits[2:]:
            for c in sorted(found):
                found[c ^ bit] = swap_dp(found[c], size, bit)
        stacked = jnp.stack([found[2 * p] for p in range(chips)], 0)
        return jnp.concatenate(
            [lax.dynamic_index_in_dim(stacked, chip ^ p, 0, keepdims=False) for p in range(chips)], 0
        )

    def scatter_column(total):
        found = {
            2 * p: lax.dynamic_slice_in_dim(total, (chip ^ p) * 2 * part, 2 * part, axis=0)[None] for p in range(chips)
        }
        for bit in reversed(bits[2:]):
            found = {c: found[c] + swap_dp(found[c ^ bit], size, bit) for c in found if not c & bit}
        far = back_far(found, cut_columns)
        return back_sum(back_total(found, far, cut_columns, glue_columns))

    def assemble(found):
        return place_pieces([found[2 * p] for p in range(chips)], chip_index, 2 * part)

    def assemble_gains(found):
        per = norm_gains.shape[1]
        count = 2 * 2 * 6 * per
        rows = []
        for p in range(chips):
            pieces = [v[z, 0, 2 * part :].reshape(-1)[:count] for v in found[2 * p] for z in range(v.shape[0])]
            rows.append(jnp.stack(pieces, 0).reshape(lines, 2, 2, 6, per).astype(F32))
        stacked = jnp.stack(rows, 0)
        stacked = jnp.stack([lax.dynamic_index_in_dim(stacked, chip ^ p, 0, keepdims=False) for p in range(chips)], 0)
        stacked = jnp.stack(
            [lax.dynamic_index_in_dim(stacked, (z - mp) % lines, 1, keepdims=False) for z in range(lines)], 2
        )
        total = stacked[:, :, :, 0] + stacked[:, :, :, 1]
        return total.transpose(3, 0, 1, 2, 4).reshape(6, width)

    def pieces(lefts, rights):
        if (2 * part) % 128 == 0:
            found = piece_grads(chip_index, lefts, rights, chips)
            found = {2 * p: found[p] for p in range(chips)}
        else:
            grad = jnp.stack([dot(lefts[i], v[:, at * n : (at + 1) * n], TN).astype(BF) for i, v, n, at in rights])
            found = {
                2 * p: lax.dynamic_slice_in_dim(grad, (chip ^ p) * 2 * part, 2 * part, axis=1) for p in range(chips)
            }
        for bit in reversed(bits[2:]):
            found = {c: found[c] + swap_dp(found[c ^ bit], size, bit) for c in found if not c & bit}
        return found

    def back_far(found, cut):
        if len(near) < 2:
            return {}
        a, b = near
        low, high = cut(found[a ^ b])
        return {"low": swap_dp(low, size, a), "high": swap_dp(high, size, b)}

    def back_total(found, far, cut, glue):
        total = found[0]
        if len(near) < 2:
            return total + swap_dp(found[near[0]], size, near[0]) if near else total
        a, b = near
        low, high = cut(found[b])
        to_b = glue(low + far["low"], high)
        low, high = cut(found[a])
        to_a = glue(low, high + far["high"])
        return {"own": total, "a": swap_dp(to_a, size, a), "b": swap_dp(to_b, size, b)}

    def back_sum(got):
        return got["own"] + got["a"] + got["b"] if isinstance(got, dict) else got

    def cut_columns(value):
        half = value.shape[-1] // 2
        return value[..., :half], value[..., half:]

    def glue_columns(low, high):
        return jnp.concatenate([low, high], -1)

    def cut_blocks(value):
        half = value.shape[0] // 2
        return value[:half], value[half:]

    def glue_blocks(low, high):
        return jnp.concatenate([low, high], 0)

    def lay(total):
        quarter = total.shape[-1] // lines
        return [total[..., z * quarter : (z + 1) * quarter] for z in range(lines)]

    def scatter_line(laid):
        return lax.psum_scatter(laid, "mp", scatter_dimension=0, tiled=True)[0]

    def scatter_shift(pieces):
        total = pieces[0].astype(F32)
        for k in range(1, lines):
            total = total + move_mp(pieces[k], [(i, (i + k) % lines) for i in range(lines)]).astype(F32)
        return total.astype(BF)

    def scatter_core(mine):
        keep = pick(mine[:, :part], mine[:, part:])
        recv = swap_core(pick(mine[:, part:], mine[:, :part]))
        return jnp.concatenate([pick(keep, recv), pick(recv, keep)], -1).astype(F32)

    items = image_states.shape[0]
    run = image_states.shape[1] // 2

    def bring_core(value):
        blocks = value.reshape(items, 2, run, width)
        keep = pick(blocks[:, 0], blocks[:, 1])
        recv = swap_core(pick(blocks[:, 1], blocks[:, 0]))
        return jnp.concatenate([pick(keep, recv), pick(recv, keep)], 0)

    def bring_line(whole):
        return lax.all_to_all(whole, "mp", 0, 0, tiled=True)

    def bring_last(whole):
        return whole.reshape(lines * run, width)

    def give_line(value, rows):
        return lax.all_to_all(value.reshape(lines, rows, width), "mp", 0, 0, tiled=True)

    def give_core(whole):
        low, high = whole[:items], whole[items:]
        keep = pick(low, high)
        recv = swap_core(pick(high, low))
        rows = whole.shape[1]
        return jnp.stack([pick(keep, recv), pick(recv, keep)], 1).reshape(items, 2 * rows, width).astype(F32)

    def both(value):
        return jnp.concatenate([value, swap_core(value)], 0)

    def joined(left, right, dims):
        half = left.shape[0] // 2
        other = dot(left[half:], right, dims).astype(BF)
        return dot(left[:half], right, dims) + swap_core(other).astype(F32)

    def sum_all(value):
        bit = 1
        while bit < size:
            value = value + swap_dp(value, size, bit)
            bit *= 2
        value = value + move_mp(value, PAIR)
        return value + move_mp(value, ACROSS)

    def sum_fast(value):
        value = value + swap_core(value)
        for i in range(0, len(bits), 2):
            pair = bits[i : i + 2]
            others = pair + [sum(pair)] if len(pair) == 2 else pair
            value = value + sum(swap_dp(value, size, b) for b in others)
        shifts = [[(i, (i + k) % lines) for i in range(lines)] for k in range(1, lines)]
        return value + sum(move_mp(value, pairs) for pairs in shifts)

    low = jnp.concatenate([input_weights[:3], output_weights[:1], input_weights[3:], output_weights[1:]], 0).astype(BF)
    own_inout = own_half(low)
    own_hidden = own_half(hidden_weights.astype(BF))
    gains_high = norm_gains.astype(BF)
    gains_low = (norm_gains - gains_high.astype(F32)).astype(BF)
    gains_own = jnp.stack([gains_high, gains_low], 0)
    gains_recv = swap_core(gains_own)
    gains_chip = jnp.stack([pick(gains_own, gains_recv), pick(gains_recv, gains_own)], 0)
    extra = -(-gains_chip.size // 1024) * 8
    gains_rows = jnp.pad(gains_chip.reshape(-1), (0, extra * 128 - gains_chip.size)).reshape(1, extra, 128)
    gains_rows = jnp.pad(gains_rows, ((0, 3), (0, 0), (0, 0)))
    own_self = jnp.concatenate([own_inout[:4], gains_rows], 1)

    def shift(value, step):
        return move_mp(value, [(i, (i - step) % lines) for i in range(lines)])

    moved = [own_self] + [shift(own_self, k) for k in range(1, lines)]
    image_core = bring_core(image_states)
    column_down = gather_column(own_hidden[1])
    moved, image_core, own_cross, column_down = tie(moved, image_core, own_inout[4:], column_down)
    self_line = jnp.stack(moved, 0)
    self_whole = phase_first(self_line)
    image_line = bring_line(image_core)
    self_whole, own_cross, image_line = tie(self_whole, own_cross, image_line)
    cross_line = lax.all_gather(own_cross, "mp", axis=0)
    found_self = whole_on(self_line, self_whole)
    image_all = both(bring_last(image_line))
    cross_line, own_up = tie(cross_line, own_hidden[:1])
    up_line = lax.all_gather(own_up, "mp", axis=0)
    cot_core = bring_core(cotangent)
    up_line, column_down, cot_core = tie(up_line, column_down, cot_core)
    weights_down = lax.all_gather(column_down, "mp", axis=0)
    cot_line = bring_line(cot_core)

    which = mp % items
    mine = lax.dynamic_index_in_dim(text_states, which, 0, keepdims=False)
    mine_mask = lax.dynamic_index_in_dim(text_mask, which, 0, keepdims=False).astype(F32)
    here = (mp // items) == core
    text = jnp.where(here, mine, swap_core(mine))
    valid = jnp.where(here, mine_mask, swap_core(mine_mask))
    valid = jnp.broadcast_to(valid[:, None], (valid.shape[0], 128))

    core_index = core.astype(jnp.int32).reshape(1)

    half = image_all.shape[0] // 2
    found_self, image_all = tie(found_self, image_all)
    weights_self = assemble(found_self)
    gain_rows = assemble_gains(found_self)
    image_float = image_all.astype(F32)
    image_own = image_float[:half]
    unit, _ = norm_parts(image_float)
    h1 = (unit * gain_rows[0] + gain_rows[1]).astype(BF)
    h1, cross_line = tie(h1, cross_line)
    cross_whole = phase_first(cross_line)
    q1, k1, v1 = (dot(h1, weights_self[j], NN).astype(BF) for j in range(3))
    o1, l1 = self_fwd(core_index, q1, k1, v1)
    o1, cross_whole = tie(o1, cross_whole)
    found_cross = whole_on(cross_line, cross_whole)
    r1 = image_own + joined(o1, weights_self[3], NT)
    unit, _ = norm_parts(r1)
    h2 = both((unit * gain_rows[2] + gain_rows[3]).astype(BF))
    h2, found_cross, up_line = tie(h2, found_cross, up_line)
    up_whole = phase_first(up_line)
    weights_cross = assemble(found_cross)
    q2 = dot(h2, weights_cross[0], NN).astype(BF)
    k2, v2 = (dot(text, weights_cross[j], NN).astype(BF) for j in (1, 2))
    o2, l2 = cross_fwd(valid, q2, k2, v2)
    o2, up_whole = tie(o2, up_whole)
    found_up = whole_on(up_line, up_whole)
    r2 = r1 + joined(o2, weights_cross[3], NT)
    unit, _ = norm_parts(r2)
    h3 = both((unit * gain_rows[4] + gain_rows[5]).astype(BF))
    h3, found_up = tie(h3, found_up)
    weights_up = place_hidden([found_up[2 * p] for p in range(chips)], chip_index, 2 * part)
    e, slope = hidden_up(h3, weights_up)
    e, slope, cot_line = tie(e, slope, cot_line)
    cot_own = bring_last(cot_line)
    cot = both(cot_own)
    cot_float = cot_own.astype(F32)
    grad_down = token_grad(cot, e, lines)
    e, slope, weights_down, grad_down = tie(e, slope, weights_down, grad_down)

    def joined_hidden(value, weights):
        other = hidden_down(value, weights, 1, BF)
        return hidden_down(value, weights, 0, F32) + swap_core(other).astype(F32)

    line_down = lax.psum_scatter(grad_down, "mp", scatter_dimension=0)
    du = hidden_slope(cot, weights_down, slope)
    send_up = pieces([h3], [(0, du, du.shape[1] // lines, z) for z in range(lines)])
    far_up = back_far(send_up, cut_blocks)
    dh3 = joined_hidden(du, weights_up)
    back, gain_five, shift_six = norm_back(r2, dh3, gain_rows[4])
    dr2 = cot_float + back
    z2 = both(dr2.astype(BF))
    z2, far_up = tie(z2, far_up)
    total_up = back_total(send_up, far_up, cut_blocks, glue_blocks)
    layer_own = r2 + joined_hidden(e, weights_down)
    do2 = dot(z2, weights_cross[3], NN).astype(BF)
    dq2, dk2, dv2 = cross_bwd(valid, q2, k2, v2, do2, l2)
    dq2, dk2, dv2, layer_own, line_down = tie(dq2, dk2, dv2, layer_own, line_down)
    near_down = scatter_column(line_down)
    layer_line = give_line(layer_own.astype(BF), run)
    dh2 = joined(dq2, weights_cross[0], NT)
    send_cross = pieces([h2, z2], [(0, dq2, dq2.shape[1], 0), (1, o2, o2.shape[1], 0)])
    gi4 = dot(text, dk2, TN).astype(BF)
    gi5 = dot(text, dv2, TN).astype(BF)
    send_text = {
        2 * p: jnp.stack(
            [lax.dynamic_slice_in_dim(v, (chip ^ p) * 2 * part, 2 * part, axis=0) for v in (gi4, gi5)]
        )
        for p in range(chips)
    }
    for bit in reversed(bits[2:]):
        send_text = {c: send_text[c] + swap_dp(send_text[c ^ bit], size, bit) for c in send_text if not c & bit}
    send_cross = {c: jnp.concatenate([send_cross[c], send_text[c]], 0) for c in send_cross}
    back, gain_three, shift_four = norm_back(r1, dh2, gain_rows[2])
    dr1 = dr2 + back
    z1 = both(dr1.astype(BF))
    z1, send_cross, total_up = tie(z1, send_cross, total_up)
    near_up = scatter_line(back_sum(total_up))[None]
    far_cross = back_far(send_cross, cut_columns)
    text_part = dot(dk2, weights_cross[1], NT) + dot(dv2, weights_cross[2], NT)
    share = text.shape[0] // (2 * lines)
    text_part = text_part.reshape(lines, 2, share, width)
    text_own = pick(text_part[:, 0], text_part[:, 1]) + swap_core(
        pick(text_part[:, 1], text_part[:, 0]).astype(BF)
    ).astype(F32)
    text_line = give_line(text_own.astype(BF).reshape(lines * share, width), share)
    do1 = dot(z1, weights_self[3], NN).astype(BF)
    do1, far_cross = tie(do1, far_cross)
    total_cross = back_total(send_cross, far_cross, cut_columns, glue_columns)
    dq1, dk1, dv1 = self_bwd(core_index, q1, k1, v1, do1, l1)
    dq1, dk1, dv1, text_line, layer_line, near_down = tie(dq1, dk1, dv1, text_line, layer_line, near_down)
    send_self = pieces([h1, z1], [(0, v, v.shape[1], 0) for v in (dq1, dk1, dv1)] + [(1, o1, o1.shape[1], 0)])
    far_self = back_far(send_self, cut_columns)
    send_self, dq1, dk1, dv1, total_cross = tie(send_self, dq1, dk1, dv1, total_cross)
    near_cross = scatter_line(jnp.stack(lay(back_sum(total_cross)), 0))

    def three(at):
        return (
            dot(dq1[at], weights_self[0], NT) + dot(dk1[at], weights_self[1], NT) + dot(dv1[at], weights_self[2], NT)
        )

    dh1 = three(slice(0, half)) + swap_core(three(slice(half, None)).astype(BF)).astype(F32)
    dh1, far_self = tie(dh1, far_self)
    total_self = back_total(send_self, far_self, cut_columns, glue_columns)
    back, gain_one, shift_two = norm_back(image_own, dh1, gain_rows[0])
    image_own_grad = (dr1 + back).astype(BF)
    gains_total = jnp.stack([gain_one, shift_two, gain_three, shift_four, gain_five, shift_six])
    image_line = give_line(image_own_grad, run)
    total_self, gains_total = tie(total_self, gains_total)
    gains_total = sum_all(gains_total)
    near_self = scatter_shift(lay(back_sum(total_self)))
    near_self, image_line, near_cross, near_up, near_down = tie(near_self, image_line, near_cross, near_up, near_down)
    shard_down = scatter_core(near_down)
    shard_up = scatter_core(near_up)
    shard_cross = scatter_core(near_cross)
    shard_self = scatter_core(near_self)
    layer_out = give_core(layer_line)
    image_gradient = give_core(image_line)
    text_gradient = give_core(text_line)
    gains_shard = lax.dynamic_slice_in_dim(
        gains_total, (dp * lines + mp) * norm_gains.shape[1], norm_gains.shape[1], 1
    )

    input_shard = jnp.concatenate([shard_self[:3], shard_cross[:1], shard_cross[2:]], 0)
    output_shard = jnp.concatenate([shard_self[3:], shard_cross[1:2]], 0)
    hidden_shard = jnp.concatenate([shard_up, shard_down], 0)
    square_total = jnp.sum(input_shard * input_shard) + jnp.sum(output_shard * output_shard)
    square_total = square_total + jnp.sum(hidden_shard * hidden_shard) + jnp.sum(gains_shard * gains_shard)
    global_norm = jnp.sqrt(sum_fast(jnp.full((8, 128), square_total)))[0, 0]
    factor = jnp.minimum(1.0, CLIP_LIMIT / (global_norm + 1e-06))
    input_updated, input_moment, input_square = adam_update(
        input_weights, input_shard, input_momentum, input_variance, factor, LEARN_RATE, WEIGHT_DECAY
    )
    output_updated, output_moment, output_square = adam_update(
        output_weights, output_shard, output_momentum, output_variance, factor, LEARN_RATE, WEIGHT_DECAY
    )
    hidden_updated, hidden_moment, hidden_square = adam_update(
        hidden_weights, hidden_shard, hidden_momentum, hidden_variance, factor, LEARN_RATE, WEIGHT_DECAY
    )
    gains_updated, gains_moment, gains_square = adam_update(
        norm_gains, gains_shard, gains_momentum, gains_variance, factor, GAIN_RATE, 0.0
    )
    return (
        layer_out, image_gradient, text_gradient, global_norm,
        input_updated, output_updated, hidden_updated, gains_updated,
        input_moment, output_moment, hidden_moment, gains_moment,
        input_square, output_square, hidden_square, gains_square,
    )


def solution(mesh):
    rows, weight, gains = P("dp", "mp", None), P(None, "dp", "mp"), P(None, ("dp", "mp"))
    return jax.shard_map(
        per_device,
        mesh=mesh,
        in_specs=(rows, P("dp", None, None), P("dp", None), rows) + (weight, weight, weight, gains) * 3,
        out_specs=(rows, rows, rows, P()) + (weight, weight, weight, gains) * 3,
        check_vma=False,
    )
```

```python
import math
import jax, jax.numpy as jnp
from jax import lax
from jax.experimental import pallas as pl
from jax.experimental.pallas import tpu as pltpu
BF=jnp.bfloat16; F32=jnp.float32
HEAD_DIM=64; MASKED=-1e30; FORWARD_ROWS=512; BACKWARD_ROWS=256; CROSS_ROWS=1024
NT=(((1,),(1,)),((),())); NN=(((1,),(0,)),((),())); TN=(((0,),(0,)),((),()))
TINY=pl.CostEstimate(flops=1,bytes_accessed=1,transcendentals=0)
def dot(a,b,dims): return lax.dot_general(a,b,dims,preferred_element_type=F32)

def place_of(block, core, half):
    return pl.multiple_of(((block % 2) ^ core) * half + (block // 2) * 128, 128)

def self_fwd_kernel(core_ref, q_ref, k_ref, v_ref, o_ref, l_ref, qs, ks, vs, *, seq):
    core=core_ref[0]; half=seq//2
    for b in range(seq//128):
        at=pl.ds(place_of(b,core,half),128); to=slice(b*128,b*128+128)
        qs[to,:]=(q_ref[at,:].astype(F32)*0.125).astype(BF)
        ks[to,:]=k_ref[at,:]
        vs[:,to]=v_ref[at,:].T
    low=lax.broadcasted_iota(jnp.int32,(1,128),1)<HEAD_DIM
    for i in range(seq//FORWARD_ROWS):
        n=(i+1)*FORWARD_ROWS
        q=qs[i*FORWARD_ROWS:n,:]
        outs=[]
        for h in range(2):
            keep=low if h==0 else ~low
            kh=jnp.where(keep,ks[0:n,:],jnp.zeros((),BF))
            s=dot(kh,q,NT)
            tri=lax.broadcasted_iota(jnp.int32,(FORWARD_ROWS,FORWARD_ROWS),0)<=lax.broadcasted_iota(jnp.int32,(FORWARD_ROWS,FORWARD_ROWS),1)
            diag=jnp.where(tri,s[n-FORWARD_ROWS:,:],MASKED)
            s=diag if n==FORWARD_ROWS else jnp.concatenate([s[:n-FORWARD_ROWS],diag],0)
            m=jnp.max(s,axis=0,keepdims=True)
            e=jnp.exp(s-m)
            t=jnp.sum(e,axis=0,keepdims=True)
            l_ref[0,h:h+1,i*FORWARD_ROWS:n]=m+jnp.log(t)
            o=dot(vs[h*64:h*64+64,0:n],e.astype(BF),NN)
            outs.append(o*(1.0/t))
        o=jnp.concatenate(outs,0).T.astype(BF)
        for j in range(FORWARD_ROWS//128):
            o_ref[pl.ds(place_of(i*(FORWARD_ROWS//128)+j,core,half),128),:]=o[j*128:j*128+128]

def self_bwd_kernel(core_ref, q_ref, k_ref, v_ref, g_ref, l_ref, dq_ref, dk_ref, dv_ref, qs, ks, vs, gs, kt, dka, dva, *, seq):
    core=core_ref[0]; half=seq//2
    for b in range(seq//128):
        at=pl.ds(place_of(b,core,half),128); to=slice(b*128,b*128+128)
        qs[to,:]=(q_ref[at,:].astype(F32)*0.125).astype(BF)
        k=k_ref[at,:]
        ks[to,:]=k
        kt[:,to]=k.T
        vs[to,:]=v_ref[at,:]
        gs[to,:]=g_ref[at,:]
    dka[...]=jnp.zeros_like(dka); dva[...]=jnp.zeros_like(dva)
    low=lax.broadcasted_iota(jnp.int32,(1,128),1)<HEAD_DIM
    zero=jnp.zeros((),BF)
    for i in range(seq//BACKWARD_ROWS):
        n=(i+1)*BACKWARD_ROWS; rows=slice(i*BACKWARD_ROWS,n)
        q=qs[rows,:]; g=gs[rows,:]
        ps=[]; dss=[]
        for h in range(2):
            keep=low if h==0 else ~low
            kh=jnp.where(keep,ks[0:n,:],zero)
            vh=jnp.where(keep,vs[0:n,:],zero)
            s=dot(kh,q,NT)
            tri=lax.broadcasted_iota(jnp.int32,(BACKWARD_ROWS,BACKWARD_ROWS),0)<=lax.broadcasted_iota(jnp.int32,(BACKWARD_ROWS,BACKWARD_ROWS),1)
            diag=jnp.where(tri,s[n-BACKWARD_ROWS:,:],MASKED)
            s=diag if n==BACKWARD_ROWS else jnp.concatenate([s[:n-BACKWARD_ROWS],diag],0)
            p=jnp.exp(s-l_ref[0,h:h+1,rows])
            dp=dot(vh,g,NT)
            delta=jnp.sum(p*dp,axis=0,keepdims=True)
            ds=(p*(dp-delta)).astype(BF)
            ps.append(p.astype(BF)); dss.append(ds)
        qa=jnp.concatenate([jnp.where(low,q,zero),jnp.where(low,zero,q)],0)
        ga=jnp.concatenate([jnp.where(low,g,zero),jnp.where(low,zero,g)],0)
        dva[0:n,:]+=dot(jnp.concatenate(ps,1),ga,NN)
        dka[0:n,:]+=dot(jnp.concatenate(dss,1),qa,NN)
        dqt=jnp.concatenate([dot(kt[0:64,0:n],dss[0],NN),dot(kt[64:128,0:n],dss[1],NN)],0)
        dq=(dqt.T*0.125).astype(BF)
        for j in range(BACKWARD_ROWS//128):
            dq_ref[pl.ds(place_of(i*(BACKWARD_ROWS//128)+j,core,half),128),:]=dq[j*128:j*128+128]
    for b in range(seq//128):
        at=pl.ds(place_of(b,core,half),128)
        dk_ref[at,:]=dka[b*128:b*128+128,:].astype(BF)
        dv_ref[at,:]=dva[b*128:b*128+128,:].astype(BF)

def cross_fwd_kernel(mask_ref, q_ref, k_ref, v_ref, o_ref, l_ref, *, seq):
    low=lax.broadcasted_iota(jnp.int32,(1,128),1)<HEAD_DIM
    zero=jnp.zeros((),BF)
    valid=mask_ref[:,0:1]>0
    k=k_ref[...]; vt=v_ref[...].T
    for i in range(seq//CROSS_ROWS):
        rows=slice(i*CROSS_ROWS,(i+1)*CROSS_ROWS)
        q=(q_ref[rows,:].astype(F32)*0.125).astype(BF)
        outs=[]
        for h in range(2):
            kh=jnp.where(low if h==0 else ~low,k,zero)
            s=jnp.where(valid,dot(kh,q,NT),MASKED)
            m=jnp.max(s,axis=0,keepdims=True)
            e=jnp.exp(s-m)
            t=jnp.sum(e,axis=0,keepdims=True)
            l_ref[0,h:h+1,rows]=m+jnp.log(t)
            outs.append(dot(vt[h*64:h*64+64,:],e.astype(BF),NN)*(1.0/t))
        o_ref[rows,:]=jnp.concatenate(outs,0).T.astype(BF)

def cross_bwd_kernel(mask_ref, q_ref, k_ref, v_ref, g_ref, l_ref, dq_ref, dk_ref, dv_ref, *, seq):
    low=lax.broadcasted_iota(jnp.int32,(1,128),1)<HEAD_DIM
    zero=jnp.zeros((),BF)
    valid=mask_ref[:,0:1]>0
    k=k_ref[...]; v=v_ref[...]; kt=k.T
    dk=jnp.zeros(k.shape,F32); dv=jnp.zeros(k.shape,F32)
    for i in range(seq//CROSS_ROWS):
        rows=slice(i*CROSS_ROWS,(i+1)*CROSS_ROWS)
        q=(q_ref[rows,:].astype(F32)*0.125).astype(BF); g=g_ref[rows,:]
        ps=[]; dss=[]; dqs=[]
        for h in range(2):
            keep=low if h==0 else ~low
            kh=jnp.where(keep,k,zero); vh=jnp.where(keep,v,zero)
            s=jnp.where(valid,dot(kh,q,NT),MASKED)
            p=jnp.exp(s-l_ref[0,h:h+1,rows])
            dp=dot(vh,g,NT)
            delta=jnp.sum(p*dp,axis=0,keepdims=True)
            ds=(p*(dp-delta)).astype(BF)
            ps.append(p.astype(BF)); dss.append(ds)
            dqs.append(dot(kt[h*64:h*64+64,:],ds,NN))
        qa=jnp.concatenate([jnp.where(low,q,zero),jnp.where(low,zero,q)],0)
        ga=jnp.concatenate([jnp.where(low,g,zero),jnp.where(low,zero,g)],0)
        dv=dv+dot(jnp.concatenate(ps,1),ga,NN)
        dk=dk+dot(jnp.concatenate(dss,1),qa,NN)
        dq_ref[rows,:]=(jnp.concatenate(dqs,0).T*0.125).astype(BF)
    dk_ref[...]=dk.astype(BF); dv_ref[...]=dv.astype(BF)

def col(rows): return pl.BlockSpec((rows,128),lambda p,*_:(0,p))
LSPEC=pl.BlockSpec((1,2,None),lambda p,*_:(p,0,0))
def params(mib=32): return pltpu.CompilerParams(vmem_limit_bytes=mib*1024*1024)
def self_fwd(core,q,k,v):
    seq,cols=q.shape; pairs=cols//128
    return pl.pallas_call(lambda *r: self_fwd_kernel(*r,seq=seq),
        grid_spec=pltpu.PrefetchScalarGridSpec(num_scalar_prefetch=1,grid=(pairs,),in_specs=[col(seq)]*3,
            out_specs=[col(seq),pl.BlockSpec((1,2,seq),lambda p,*_:(p,0,0))],scratch_shapes=[pltpu.VMEM((seq,128),BF)]*2+[pltpu.VMEM((128,seq),BF)]),
        out_shape=[jax.ShapeDtypeStruct((seq,cols),BF),jax.ShapeDtypeStruct((pairs,2,seq),F32)],
        compiler_params=params(),
        cost_estimate=TINY,name="self_forward")(core,q,k,v)
def self_bwd(core,q,k,v,g,l):
    seq,cols=q.shape; pairs=cols//128
    return pl.pallas_call(lambda *r: self_bwd_kernel(*r,seq=seq),
        grid_spec=pltpu.PrefetchScalarGridSpec(num_scalar_prefetch=1,grid=(pairs,),in_specs=[col(seq)]*4+[pl.BlockSpec((1,2,seq),lambda p,*_:(p,0,0))],
            out_specs=[col(seq)]*3,scratch_shapes=[pltpu.VMEM((seq,128),BF)]*4+[pltpu.VMEM((128,seq),BF)]+[pltpu.VMEM((seq,128),F32)]*2),
        out_shape=[jax.ShapeDtypeStruct((seq,cols),BF)]*3,
        compiler_params=params(),
        cost_estimate=TINY,name="self_backward")(core,q,k,v,g,l)
def cross_fwd(mask,q,k,v):
    seq,cols=q.shape; text=k.shape[0]; pairs=cols//128
    return pl.pallas_call(lambda *r: cross_fwd_kernel(*r,seq=seq),grid=(pairs,),
        in_specs=[pl.BlockSpec((text,128),lambda p:(0,0)),col(seq),col(text),col(text)],
        out_specs=[col(seq),pl.BlockSpec((1,2,seq),lambda p:(p,0,0))],
        out_shape=[jax.ShapeDtypeStruct((seq,cols),BF),jax.ShapeDtypeStruct((pairs,2,seq),F32)],
        compiler_params=params(),
        cost_estimate=TINY,name="cross_forward")(mask,q,k,v)
def cross_bwd(mask,q,k,v,g,l):
    seq,cols=q.shape; text=k.shape[0]; pairs=cols//128
    return pl.pallas_call(lambda *r: cross_bwd_kernel(*r,seq=seq),grid=(pairs,),
        in_specs=[pl.BlockSpec((text,128),lambda p:(0,0)),col(seq),col(text),col(text),col(seq),pl.BlockSpec((1,2,seq),lambda p:(p,0,0))],
        out_specs=[col(seq),col(text),col(text)],
        out_shape=[jax.ShapeDtypeStruct((seq,cols),BF),jax.ShapeDtypeStruct((text,cols),BF),jax.ShapeDtypeStruct((text,cols),BF)],
        compiler_params=params(),
        cost_estimate=TINY,name="cross_backward")(mask,q,k,v,g,l)

def split_halves(a,b):
    half,m,rows,cols=a.shape[0]//2,*a.shape[1:]
    def body(a_ref,b_ref,x_ref,y_ref):
        x_ref[...]=a_ref[...]
        y_ref[...]=b_ref[...]
    block=(half,1,rows,cols)
    out=jax.ShapeDtypeStruct((half,m,rows,cols),a.dtype)
    return pl.pallas_call(body,grid=(m,),
        in_specs=[pl.BlockSpec(block,lambda i:(0,i,0,0)),pl.BlockSpec(block,lambda i:(1,i,0,0))],
        out_specs=[pl.BlockSpec(block,lambda i:(0,i,0,0))]*2,out_shape=[out,out],compiler_params=params(),
        cost_estimate=TINY,name="split_halves")(a,b)

def place_pieces(groups,chip,rows):
    first=groups[0][0]
    _,m,_,cols=first.shape
    width=sum(v.shape[0] for v in groups[0])*cols
    flat=[v for g in groups for v in g]
    shapes=[[v.shape[0] for v in g] for g in groups]
    def body(chip_ref,*refs):
        ins,out=refs[:len(flat)],refs[len(flat)]
        at=0
        for p,s in enumerate(shapes):
            def fill(at=at,s=s):
                z=0
                for i,k in enumerate(s):
                    for j in range(k):
                        out[:,:,z*cols:(z+1)*cols]=ins[at+i][j,:,0:rows,:]; z+=1
            pl.when(pl.program_id(0)==p)(fill)
            at+=len(s)
    return pl.pallas_call(body,
        grid_spec=pltpu.PrefetchScalarGridSpec(num_scalar_prefetch=1,grid=(len(groups),),
            in_specs=[pl.BlockSpec(v.shape,lambda p,c:(0,0,0,0),pipeline_mode=pl.Buffered(1)) for v in flat],
            out_specs=pl.BlockSpec((m,rows,width),lambda p,c:(0,p^c[0],0))),
        out_shape=jax.ShapeDtypeStruct((m,rows*len(groups),width),first.dtype),compiler_params=params(),
        cost_estimate=TINY,name="place_pieces")(chip,*flat)

def hidden_up_kernel(h_ref, w_ref, e_ref, s_ref):
    w=w_ref[0]
    for i in range(h_ref.shape[0]//256):
        rows=slice(i*256,(i+1)*256)
        u=dot(h_ref[rows,:],w,NN)
        uu=u*u
        t=jnp.tanh(u*(0.7978845608028654+(0.7978845608028654*0.044715)*uu))
        p=0.5+0.5*t
        e_ref[rows,:]=(u*p).astype(BF)
        s_ref[rows,:]=(p+u*(p*(1.0-t))*(0.7978845608028654+(3.0*0.7978845608028654*0.044715)*uu)).astype(BF)

def hidden_up(h,w):
    rows,depth=h.shape; parts,_,cols=w.shape; blk=256; per=cols//blk
    out=pl.BlockSpec((rows,blk),lambda j:(0,j))
    return pl.pallas_call(hidden_up_kernel,grid=(parts*per,),
        in_specs=[pl.BlockSpec((rows,depth),lambda j:(0,0)),pl.BlockSpec((1,depth,blk),lambda j:(j//per,0,j%per))],
        out_specs=[out,out],out_shape=[jax.ShapeDtypeStruct((rows,parts*cols),BF)]*2,compiler_params=params(),
        cost_estimate=TINY,name="hidden_up")(h,w)

def hidden_slope_kernel(g_ref, w_ref, s_ref, d_ref):
    w=w_ref[0]
    for i in range(g_ref.shape[0]//256):
        rows=slice(i*256,(i+1)*256)
        d_ref[rows,:]=(dot(g_ref[rows,:],w,NN)*s_ref[rows,:].astype(F32)).astype(BF)

def hidden_slope(g,w,s):
    rows,depth=g.shape; parts,_,cols=w.shape; blk=256; per=cols//blk
    out=pl.BlockSpec((rows,blk),lambda j:(0,j))
    return pl.pallas_call(hidden_slope_kernel,grid=(parts*per,),
        in_specs=[pl.BlockSpec((rows,depth),lambda j:(0,0)),pl.BlockSpec((1,depth,blk),lambda j:(j//per,0,j%per)),out],
        out_specs=out,out_shape=jax.ShapeDtypeStruct((rows,parts*cols),BF),compiler_params=params(),
        cost_estimate=TINY,name="hidden_slope")(g,w,s)

def hidden_down_kernel(a_ref, w_ref, y_ref):
    cols=w_ref.shape[2]
    total=dot(a_ref[:,0:cols],w_ref[0],NT)
    for z in range(1,w_ref.shape[0]):
        total=total+dot(a_ref[:,z*cols:(z+1)*cols],w_ref[z],NT)
    y_ref[...]=total.astype(y_ref.dtype)

def hidden_down(a,w,half,kind):
    rows=a.shape[0]//2; parts,depth,cols=w.shape; blk=256
    return pl.pallas_call(hidden_down_kernel,grid=(depth//blk,),
        in_specs=[pl.BlockSpec((rows,parts*cols),lambda j:(half,0)),pl.BlockSpec((parts,blk,cols),lambda j:(0,j,0))],
        out_specs=pl.BlockSpec((rows,blk),lambda j:(0,j)),out_shape=jax.ShapeDtypeStruct((rows,depth),kind),compiler_params=params(),
        cost_estimate=TINY,name="hidden_down")(a,w)


def place_hidden(groups,chip,rows):
    first=groups[0][0]
    cols=first.shape[3]
    parts=sum(v.shape[0] for v in groups[0])
    flat=[v for g in groups for v in g]
    shapes=[[v.shape[0] for v in g] for g in groups]
    def body(chip_ref,*refs):
        ins,out=refs[:len(flat)],refs[len(flat)]
        at=0
        for p,s in enumerate(shapes):
            def fill(at=at,s=s):
                z=0
                for i,k in enumerate(s):
                    out[z:z+k]=ins[at+i][:,0]; z+=k
            pl.when(pl.program_id(0)==p)(fill)
            at+=len(s)
    return pl.pallas_call(body,
        grid_spec=pltpu.PrefetchScalarGridSpec(num_scalar_prefetch=1,grid=(len(groups),),
            in_specs=[pl.BlockSpec(v.shape,lambda p,c:(0,0,0,0),pipeline_mode=pl.Buffered(1)) for v in flat],
            out_specs=pl.BlockSpec((parts,rows,cols),lambda p,c:(0,p^c[0],0))),
        out_shape=jax.ShapeDtypeStruct((parts,rows*len(groups),cols),first.dtype),compiler_params=params(),
        cost_estimate=TINY,name="place_hidden")(chip,*flat)

def piece_grads(chip,lefts,rights,chips):
    tokens,depth=lefts[0].shape
    rows=depth//chips; m=len(rights); cols=rights[0][2]
    arrays=[]
    for _,v,_,_ in rights:
        if not any(v is w for w in arrays): arrays.append(v)
    where=[next(i for i,w in enumerate(arrays) if w is v) for _,v,_,_ in rights]
    nl,na=len(lefts),len(arrays)
    def body(chip_ref,*refs):
        ls,rs,outs=refs[:nl],refs[nl:nl+na],refs[nl+na:]
        turned=[l[...].T for l in ls]
        got=[]
        for j,(left,_,_,at) in enumerate(rights):
            r=rs[where[j]][:,at*cols:(at+1)*cols]
            got.append(dot(turned[left],r,NN).astype(BF))
        for p in range(chips):
            def fill(p=p):
                for j in range(m): outs[p][j]=got[j]
            pl.when(pl.program_id(0)==p)(fill)
    shape=jax.ShapeDtypeStruct((m,rows,cols),BF)
    return pl.pallas_call(body,
        grid_spec=pltpu.PrefetchScalarGridSpec(num_scalar_prefetch=1,grid=(chips,),
            in_specs=[pl.BlockSpec((tokens,rows),lambda p,c:(0,p^c[0])) for _ in lefts]
                +[pl.BlockSpec(v.shape,lambda p,c:(0,0),pipeline_mode=pl.Buffered(1)) for v in arrays],
            out_specs=[pl.BlockSpec((m,rows,cols),lambda p,c:(0,0,0))]*chips),
        out_shape=[shape]*chips,compiler_params=params(),cost_estimate=TINY,name="piece_grads")(chip,*lefts,*arrays)

def token_grad(a,b,parts):
    rows,depth=a.shape; cols=b.shape[1]//parts; blk=256
    def body(a_ref,b_ref,g_ref):
        turned=a_ref[...].T
        for z in range(parts):
            g_ref[z]=dot(turned,b_ref[:,z*cols:(z+1)*cols],NN).astype(BF)
    return pl.pallas_call(body,grid=(depth//blk,),
        in_specs=[pl.BlockSpec((rows,blk),lambda j:(0,j)),pl.BlockSpec(b.shape,lambda j:(0,0),pipeline_mode=pl.Buffered(1))],
        out_specs=pl.BlockSpec((parts,blk,cols),lambda j:(0,j,0)),out_shape=jax.ShapeDtypeStruct((parts,depth,cols),BF),compiler_params=params(),
        cost_estimate=TINY,name="token_grad")(a,b)


from jax.sharding import PartitionSpec as P

STEP=10
NORM_EPSILON = 1e-05
BETA_FIRST = 0.9
BETA_SECOND = 0.95
LEARN_RATE = 0.1
GAIN_RATE = 0.5
WEIGHT_DECAY = 0.1
ADAM_EPSILON = 1e-08
CLIP_LIMIT = 1.0
GELU_SCALE = 0.7978845608028654
GELU_CUBIC = 0.044715

PAIR = [(0, 1), (1, 0), (2, 3), (3, 2)]
MIDDLE = [(1, 2), (2, 1)]
OUTWARD = [(1, 0), (2, 3)]
INWARD = [(0, 1), (3, 2)]
ACROSS = [(0, 2), (1, 3), (2, 0), (3, 1)]


def tie(*values):
    return lax.optimization_barrier(values)


def swap_dp(value, size, bit):
    return lax.ppermute(value, "dp", [(i, i ^ bit) for i in range(size)])


def move_mp(value, pairs):
    return lax.ppermute(value, "mp", pairs)


def adam_update(master, gradient, momentum, variance, factor, rate, decay_rate):
    clipped = gradient * factor
    moment = BETA_FIRST * momentum + (1.0 - BETA_FIRST) * clipped
    square = BETA_SECOND * variance + (1.0 - BETA_SECOND) * clipped * clipped
    step_ratio = (
        moment
        / (1.0 - BETA_FIRST**STEP)
        / (jnp.sqrt(square / (1.0 - BETA_SECOND**STEP)) + ADAM_EPSILON)
    )
    return (master - rate * (step_ratio + decay_rate * master), moment, square)


def norm_parts(values):
    center = values - jnp.mean(values, axis=-1, keepdims=True)
    spread = jnp.mean(center * center, axis=-1, keepdims=True)
    scale = lax.rsqrt(spread + NORM_EPSILON)
    return center * scale, scale


def norm_back(values, grad, gain_row):
    unit, scale = norm_parts(values)
    scaled = grad * gain_row
    back = scale * (
        scaled
        - jnp.mean(scaled, axis=-1, keepdims=True)
        - unit * jnp.mean(scaled * unit, axis=-1, keepdims=True)
    )
    return back, jnp.sum(grad * unit, axis=0), jnp.sum(grad, axis=0)


def per_device(
    image_states, text_states, text_mask, cotangent,
    input_weights, output_weights, hidden_weights, norm_gains,
    input_momentum, output_momentum, hidden_momentum, gains_momentum,
    input_variance, output_variance, hidden_variance, gains_variance,
):
    size = lax.axis_size("dp")
    lines = lax.axis_size("mp")
    dp = lax.axis_index("dp")
    mp = lax.axis_index("mp")
    core = dp % 2
    chip = dp // 2
    chips = size // 2
    middle = (mp == 1) | (mp == 2)
    bits = []
    bit = 2
    while bit < size:
        bits.append(bit)
        bit *= 2
    width = image_states.shape[-1]
    block = width // chips
    part = width // size

    def pick(first, second):
        return jnp.where(core == 0, first, second)

    def swap_core(value):
        return swap_dp(value, size, 1)

    chip_index = chip.astype(jnp.int32).reshape(1)
    groups = [[d * lines + m for m in range(lines) for d in range(c, size, 2)] for c in range(2)]

    def own_half(stack):
        half = stack.shape[-1] // 2
        keep = lax.dynamic_slice_in_dim(stack, core * half, half, 2)
        send = lax.dynamic_slice_in_dim(stack, (1 - core) * half, half, 2)
        recv = swap_core(send)
        return jnp.concatenate([pick(keep, recv), pick(recv, keep)], 1)

    pairs = [bits[i : i + 2] for i in range(0, len(bits), 2)]

    near = pairs[0] if pairs else []

    def phase_first(line):
        return {b: swap_dp(line, size, b) for b in near}

    def whole_on(line, wholes):
        found = {0: (line,)}
        for b in near:
            found[b] = (wholes[b],)
        if len(near) == 2:
            a, b = near
            low, high = split_halves(wholes[b], wholes[a])
            found[a ^ b] = (swap_dp(low, size, a), swap_dp(high, size, b))
        for bit in bits[2:]:
            for c in sorted(found):
                found[c ^ bit] = tuple(swap_dp(v, size, bit) for v in found[c])
        return found

    def gather_column(own):
        found = {0: own}
        if len(near) == 2:
            a, b = near
            found[a], found[b] = swap_dp(own, size, a), swap_dp(own, size, b)
            found[a ^ b] = jnp.concatenate([swap_dp(found[b][:part], size, a), swap_dp(found[a][part:], size, b)], 0)
        else:
            for a in near:
                found[a] = swap_dp(own, size, a)
        for bit in bits[2:]:
            for c in sorted(found):
                found[c ^ bit] = swap_dp(found[c], size, bit)
        stacked = jnp.stack([found[2 * p] for p in range(chips)], 0)
        return jnp.concatenate(
            [lax.dynamic_index_in_dim(stacked, chip ^ p, 0, keepdims=False) for p in range(chips)], 0
        )

    def scatter_column(total):
        found = {
            2 * p: lax.dynamic_slice_in_dim(total, (chip ^ p) * 2 * part, 2 * part, axis=0)[None] for p in range(chips)
        }
        for bit in reversed(bits[2:]):
            found = {c: found[c] + swap_dp(found[c ^ bit], size, bit) for c in found if not c & bit}
        far = back_far(found, cut_columns)
        return back_sum(back_total(found, far, cut_columns, glue_columns))

    def assemble(found):
        return place_pieces([found[2 * p] for p in range(chips)], chip_index, 2 * part)

    def assemble_gains(found):
        per = norm_gains.shape[1]
        count = 2 * 2 * 6 * per
        rows = []
        for p in range(chips):
            pieces = [v[z, 0, 2 * part :].reshape(-1)[:count] for v in found[2 * p] for z in range(v.shape[0])]
            rows.append(jnp.stack(pieces, 0).reshape(lines, 2, 2, 6, per).astype(F32))
        stacked = jnp.stack(rows, 0)
        stacked = jnp.stack([lax.dynamic_index_in_dim(stacked, chip ^ p, 0, keepdims=False) for p in range(chips)], 0)
        stacked = jnp.stack(
            [lax.dynamic_index_in_dim(stacked, (z - mp) % lines, 1, keepdims=False) for z in range(lines)], 2
        )
        total = stacked[:, :, :, 0] + stacked[:, :, :, 1]
        return total.transpose(3, 0, 1, 2, 4).reshape(6, width)

    def pieces(lefts, rights):
        if (2 * part) % 128 == 0:
            found = piece_grads(chip_index, lefts, rights, chips)
            found = {2 * p: found[p] for p in range(chips)}
        else:
            grad = jnp.stack([dot(lefts[i], v[:, at * n : (at + 1) * n], TN).astype(BF) for i, v, n, at in rights])
            found = {
                2 * p: lax.dynamic_slice_in_dim(grad, (chip ^ p) * 2 * part, 2 * part, axis=1) for p in range(chips)
            }
        for bit in reversed(bits[2:]):
            found = {c: found[c] + swap_dp(found[c ^ bit], size, bit) for c in found if not c & bit}
        return found

    def back_far(found, cut):
        if len(near) < 2:
            return {}
        a, b = near
        low, high = cut(found[a ^ b])
        return {"low": swap_dp(low, size, a), "high": swap_dp(high, size, b)}

    def back_total(found, far, cut, glue):
        total = found[0]
        if len(near) < 2:
            return total + swap_dp(found[near[0]], size, near[0]) if near else total
        a, b = near
        low, high = cut(found[b])
        to_b = glue(low + far["low"], high)
        low, high = cut(found[a])
        to_a = glue(low, high + far["high"])
        return {"own": total, "a": swap_dp(to_a, size, a), "b": swap_dp(to_b, size, b)}

    def back_sum(got):
        return got["own"] + got["a"] + got["b"] if isinstance(got, dict) else got

    def cut_columns(value):
        half = value.shape[-1] // 2
        return value[..., :half], value[..., half:]

    def glue_columns(low, high):
        return jnp.concatenate([low, high], -1)

    def cut_blocks(value):
        half = value.shape[0] // 2
        return value[:half], value[half:]

    def glue_blocks(low, high):
        return jnp.concatenate([low, high], 0)

    def lay(total):
        quarter = total.shape[-1] // lines
        return [total[..., z * quarter : (z + 1) * quarter] for z in range(lines)]

    def scatter_line(laid):
        return lax.psum_scatter(laid, "mp", scatter_dimension=0, tiled=True)[0]

    def scatter_shift(pieces):
        total = pieces[0].astype(F32)
        for k in range(1, lines):
            total = total + move_mp(pieces[k], [(i, (i + k) % lines) for i in range(lines)]).astype(F32)
        return total.astype(BF)

    def scatter_core(mine):
        keep = pick(mine[:, :part], mine[:, part:])
        recv = swap_core(pick(mine[:, part:], mine[:, :part]))
        return jnp.concatenate([pick(keep, recv), pick(recv, keep)], -1).astype(F32)

    items = image_states.shape[0]
    run = image_states.shape[1] // 2

    def bring_core(value):
        blocks = value.reshape(items, 2, run, width)
        keep = pick(blocks[:, 0], blocks[:, 1])
        recv = swap_core(pick(blocks[:, 1], blocks[:, 0]))
        return jnp.concatenate([pick(keep, recv), pick(recv, keep)], 0)

    def bring_line(whole):
        return lax.all_to_all(whole, "mp", 0, 0, tiled=True)

    def bring_last(whole):
        return whole.reshape(lines * run, width)

    def give_line(value, rows):
        return lax.all_to_all(value.reshape(lines, rows, width), "mp", 0, 0, tiled=True)

    def give_core(whole):
        low, high = whole[:items], whole[items:]
        keep = pick(low, high)
        recv = swap_core(pick(high, low))
        rows = whole.shape[1]
        return jnp.stack([pick(keep, recv), pick(recv, keep)], 1).reshape(items, 2 * rows, width).astype(F32)

    def both(value):
        return jnp.concatenate([value, swap_core(value)], 0)

    def joined(left, right, dims):
        half = left.shape[0] // 2
        other = dot(left[half:], right, dims).astype(BF)
        return dot(left[:half], right, dims) + swap_core(other).astype(F32)

    def sum_chips(value):
        value = value + swap_core(value)
        for i in range(0, len(bits), 2):
            pair = bits[i : i + 2]
            others = pair + [sum(pair)] if len(pair) == 2 else pair
            value = value + sum(swap_dp(value, size, b) for b in others)
        return value

    def sum_line(value):
        shifts = [[(i, (i + k) % lines) for i in range(lines)] for k in range(1, lines)]
        return value + sum(move_mp(value, pairs) for pairs in shifts)

    low = jnp.concatenate([input_weights[:3], output_weights[:1], input_weights[3:], output_weights[1:]], 0).astype(BF)
    own_inout = own_half(low)
    own_hidden = own_half(hidden_weights.astype(BF))
    gains_high = norm_gains.astype(BF)
    gains_low = (norm_gains - gains_high.astype(F32)).astype(BF)
    gains_own = jnp.stack([gains_high, gains_low], 0)
    gains_recv = swap_core(gains_own)
    gains_chip = jnp.stack([pick(gains_own, gains_recv), pick(gains_recv, gains_own)], 0)
    extra = -(-gains_chip.size // 1024) * 8
    gains_rows = jnp.pad(gains_chip.reshape(-1), (0, extra * 128 - gains_chip.size)).reshape(1, extra, 128)
    gains_rows = jnp.pad(gains_rows, ((0, 3), (0, 0), (0, 0)))
    own_self = jnp.concatenate([own_inout[:4], gains_rows], 1)

    def shift(value, step):
        return move_mp(value, [(i, (i - step) % lines) for i in range(lines)])

    moved = [own_self] + [shift(own_self, k) for k in range(1, lines)]
    image_core = bring_core(image_states)
    column_down = gather_column(own_hidden[1])
    moved, image_core, own_cross, column_down = tie(moved, image_core, own_inout[4:], column_down)
    self_line = jnp.stack(moved, 0)
    self_whole = phase_first(self_line)
    image_line = bring_line(image_core)
    cross_line = lax.all_gather(own_cross, "mp", axis=0)
    found_self = whole_on(self_line, self_whole)
    found_self, image_line, cross_line = tie(found_self, image_line, cross_line)
    image_all = both(bring_last(image_line))
    cross_line, own_up = tie(cross_line, own_hidden[:1])
    up_line = lax.all_gather(own_up, "mp", axis=0)
    cot_core = bring_core(cotangent)

    which = mp % items
    mine = lax.dynamic_index_in_dim(text_states, which, 0, keepdims=False)
    mine_mask = lax.dynamic_index_in_dim(text_mask, which, 0, keepdims=False).astype(F32)
    here = (mp // items) == core
    text = jnp.where(here, mine, swap_core(mine))
    valid = jnp.where(here, mine_mask, swap_core(mine_mask))
    valid = jnp.broadcast_to(valid[:, None], (valid.shape[0], 128))

    core_index = core.astype(jnp.int32).reshape(1)

    half = image_all.shape[0] // 2
    weights_self = assemble(found_self)
    gain_rows = assemble_gains(found_self)
    image_float = image_all.astype(F32)
    image_own = image_float[:half]
    unit, _ = norm_parts(image_float)
    h1 = (unit * gain_rows[0] + gain_rows[1]).astype(BF)
    cross_whole = phase_first(cross_line)
    q1, k1, v1 = (dot(h1, weights_self[j], NN).astype(BF) for j in range(3))
    o1, l1 = self_fwd(core_index, q1, k1, v1)
    o1, cross_whole, up_line, column_down, cot_core = tie(o1, cross_whole, up_line, column_down, cot_core)
    cot_line = bring_line(cot_core)
    weights_down = lax.all_gather(column_down, "mp", axis=0)
    found_cross = whole_on(cross_line, cross_whole)
    r1 = image_own + joined(o1, weights_self[3], NT)
    unit, _ = norm_parts(r1)
    h2 = both((unit * gain_rows[2] + gain_rows[3]).astype(BF))
    h2, found_cross = tie(h2, found_cross)
    up_whole = phase_first(up_line)
    weights_cross = assemble(found_cross)
    q2 = dot(h2, weights_cross[0], NN).astype(BF)
    k2, v2 = (dot(text, weights_cross[j], NN).astype(BF) for j in (1, 2))
    o2, l2 = cross_fwd(valid, q2, k2, v2)
    o2, up_whole, cot_line = tie(o2, up_whole, cot_line)
    found_up = whole_on(up_line, up_whole)
    r2 = r1 + joined(o2, weights_cross[3], NT)
    unit, _ = norm_parts(r2)
    h3 = both((unit * gain_rows[4] + gain_rows[5]).astype(BF))
    h3, found_up = tie(h3, found_up)
    weights_up = place_hidden([found_up[2 * p] for p in range(chips)], chip_index, 2 * part)
    e, slope = hidden_up(h3, weights_up)
    e, slope, cot_line = tie(e, slope, cot_line)
    cot_own = bring_last(cot_line)
    cot = both(cot_own)
    cot_float = cot_own.astype(F32)
    grad_down = token_grad(cot, e, lines)
    e, slope, weights_down, grad_down = tie(e, slope, weights_down, grad_down)

    def joined_hidden(value, weights):
        other = hidden_down(value, weights, 1, BF)
        return hidden_down(value, weights, 0, F32) + swap_core(other).astype(F32)

    line_down = lax.psum_scatter(grad_down, "mp", scatter_dimension=0)
    du = hidden_slope(cot, weights_down, slope)
    send_up = pieces([h3], [(0, du, du.shape[1] // lines, z) for z in range(lines)])
    far_up = back_far(send_up, cut_blocks)
    dh3 = joined_hidden(du, weights_up)
    back, gain_five, shift_six = norm_back(r2, dh3, gain_rows[4])
    dr2 = cot_float + back
    z2 = both(dr2.astype(BF))
    z2, far_up = tie(z2, far_up)
    total_up = back_total(send_up, far_up, cut_blocks, glue_blocks)
    layer_own = r2 + joined_hidden(e, weights_down)
    do2 = dot(z2, weights_cross[3], NN).astype(BF)
    dq2, dk2, dv2 = cross_bwd(valid, q2, k2, v2, do2, l2)
    dq2, dk2, dv2, layer_own, line_down = tie(dq2, dk2, dv2, layer_own, line_down)
    near_down = scatter_column(line_down)
    layer_line = give_line(layer_own.astype(BF), run)
    dh2 = joined(dq2, weights_cross[0], NT)
    send_cross = pieces([h2, z2], [(0, dq2, dq2.shape[1], 0), (1, o2, o2.shape[1], 0)])
    gi4 = dot(text, dk2, TN).astype(BF)
    gi5 = dot(text, dv2, TN).astype(BF)
    send_text = {
        2 * p: jnp.stack(
            [lax.dynamic_slice_in_dim(v, (chip ^ p) * 2 * part, 2 * part, axis=0) for v in (gi4, gi5)]
        )
        for p in range(chips)
    }
    for bit in reversed(bits[2:]):
        send_text = {c: send_text[c] + swap_dp(send_text[c ^ bit], size, bit) for c in send_text if not c & bit}
    send_cross = {c: jnp.concatenate([send_cross[c], send_text[c]], 0) for c in send_cross}
    back, gain_three, shift_four = norm_back(r1, dh2, gain_rows[2])
    dr1 = dr2 + back
    z1 = both(dr1.astype(BF))
    z1, send_cross, total_up = tie(z1, send_cross, total_up)
    near_up = scatter_line(back_sum(total_up))[None]
    far_cross = back_far(send_cross, cut_columns)
    text_part = dot(dk2, weights_cross[1], NT) + dot(dv2, weights_cross[2], NT)
    share = text.shape[0] // (2 * lines)
    text_part = text_part.reshape(lines, 2, share, width)
    text_own = pick(text_part[:, 0], text_part[:, 1]) + swap_core(
        pick(text_part[:, 1], text_part[:, 0]).astype(BF)
    ).astype(F32)
    text_line = give_line(text_own.astype(BF).reshape(lines * share, width), share)
    do1 = dot(z1, weights_self[3], NN).astype(BF)
    do1, far_cross = tie(do1, far_cross)
    total_cross = back_total(send_cross, far_cross, cut_columns, glue_columns)
    dq1, dk1, dv1 = self_bwd(core_index, q1, k1, v1, do1, l1)
    dq1, dk1, dv1, near_down = tie(dq1, dk1, dv1, near_down)
    send_self = pieces([h1, z1], [(0, v, v.shape[1], 0) for v in (dq1, dk1, dv1)] + [(1, o1, o1.shape[1], 0)])
    far_self = back_far(send_self, cut_columns)
    send_self, dq1, dk1, dv1, total_cross = tie(send_self, dq1, dk1, dv1, total_cross)
    near_cross = scatter_line(jnp.stack(lay(back_sum(total_cross)), 0))

    def three(at):
        return (
            dot(dq1[at], weights_self[0], NT) + dot(dk1[at], weights_self[1], NT) + dot(dv1[at], weights_self[2], NT)
        )

    dh1 = three(slice(0, half)) + swap_core(three(slice(half, None)).astype(BF)).astype(F32)
    dh1, far_self = tie(dh1, far_self)
    total_self = back_total(send_self, far_self, cut_columns, glue_columns)
    back, gain_one, shift_two = norm_back(image_own, dh1, gain_rows[0])
    image_own_grad = (dr1 + back).astype(BF)
    gains_total = jnp.stack([gain_one, shift_two, gain_three, shift_four, gain_five, shift_six])
    gains_total = sum_line(gains_total)
    gains_total, image_own_grad = tie(gains_total, image_own_grad)
    image_line = give_line(image_own_grad, run)
    total_self, gains_total = tie(total_self, gains_total)
    gains_total = sum_chips(gains_total)
    near_self = scatter_shift(lay(back_sum(total_self)))
    near_self, image_line, near_cross, near_up, near_down = tie(near_self, image_line, near_cross, near_up, near_down)
    shard_down = scatter_core(near_down)
    shard_up = scatter_core(near_up)
    shard_cross = scatter_core(near_cross)
    shard_self = scatter_core(near_self)
    layer_out = give_core(layer_line)
    image_gradient = give_core(image_line)
    text_gradient = give_core(text_line)
    gains_shard = lax.dynamic_slice_in_dim(
        gains_total, (dp * lines + mp) * norm_gains.shape[1], norm_gains.shape[1], 1
    )

    input_shard = jnp.concatenate([shard_self[:3], shard_cross[:1], shard_cross[2:]], 0)
    output_shard = jnp.concatenate([shard_self[3:], shard_cross[1:2]], 0)
    hidden_shard = jnp.concatenate([shard_up, shard_down], 0)
    square_total = jnp.sum(input_shard * input_shard) + jnp.sum(output_shard * output_shard)
    square_total = square_total + jnp.sum(hidden_shard * hidden_shard) + jnp.sum(gains_shard * gains_shard)
    global_norm = jnp.sqrt(sum_line(sum_chips(jnp.full((8, 128), square_total))))[0, 0]
    factor = jnp.minimum(1.0, CLIP_LIMIT / (global_norm + 1e-06))
    input_updated, input_moment, input_square = adam_update(
        input_weights, input_shard, input_momentum, input_variance, factor, LEARN_RATE, WEIGHT_DECAY
    )
    output_updated, output_moment, output_square = adam_update(
        output_weights, output_shard, output_momentum, output_variance, factor, LEARN_RATE, WEIGHT_DECAY
    )
    hidden_updated, hidden_moment, hidden_square = adam_update(
        hidden_weights, hidden_shard, hidden_momentum, hidden_variance, factor, LEARN_RATE, WEIGHT_DECAY
    )
    gains_updated, gains_moment, gains_square = adam_update(
        norm_gains, gains_shard, gains_momentum, gains_variance, factor, GAIN_RATE, 0.0
    )
    return (
        layer_out, image_gradient, text_gradient, global_norm,
        input_updated, output_updated, hidden_updated, gains_updated,
        input_moment, output_moment, hidden_moment, gains_moment,
        input_square, output_square, hidden_square, gains_square,
    )


def solution(mesh):
    rows, weight, gains = P("dp", "mp", None), P(None, "dp", "mp"), P(None, ("dp", "mp"))
    return jax.shard_map(
        per_device,
        mesh=mesh,
        in_specs=(rows, P("dp", None, None), P("dp", None), rows) + (weight, weight, weight, gains) * 3,
        out_specs=(rows, rows, rows, P()) + (weight, weight, weight, gains) * 3,
        check_vma=False,
    )
```
